32 devices in a mesh: dom: 4 (over y, x), gx: 4 (over z), gy: 2 (over core).
Axes of the slice: x: 2, y: 2, z: 4, core: 2. Of those that a mesh axis runs over, the one named last changes fastest.
Arguments:
- ensemble: float32 [4, 4, 32, 32, 256], P('dom', None, None, 'gx', 'gy'), may hold values from -6 to 6
- ancestors: int32 [4, 4, 32], P(None, 'gx', 'gy'), may hold values from 0 to 3
- particle_air_drag: float32 [4, 2, 32, 256], P('dom', None, 'gx', 'gy'), may hold values from -6 to 6
- eddy_diffusivity: float32 [31], replicated, may hold values from 0.02 to 0.15
Outputs:
- forecast: float32 [4, 4, 32, 32, 256], P('dom', None, None, 'gx', 'gy')
The draws below stay inside these ranges and needn't reach their ends.
All inputs are finite; a program needn't handle non-finite values.
Results may differ from the reference program's by a relative error of at most 0.0003.
Values sent between devices are 32-bit elements; how exact they have to be, the bound alone decides.
A program may use at most 64 MiB of HBM per device.

```python
import math
import jax
import jax.numpy as jnp
import numpy as np
from jax import lax

FIELDS = 4
LEV = 32
STEPS = 4
TILE = 8
PARTICLES = 4
NX = 32
NY = 256
TILES_X = 4
TILES_Y = 32


def touch_ends(result, own_key, smallest, largest):
    spot = [jax.random.randint(jax.random.fold_in(own_key, axis), (), 0, length) for axis, length in enumerate(result.shape)]
    widest = result.shape.index(max(result.shape))
    neighbour = spot[:widest] + [(spot[widest] + 1) % result.shape[widest]] + spot[widest + 1:]
    return result.at[tuple(spot)].set(smallest).at[tuple(neighbour)].set(largest)


def level_of(key, extent, cuts, smallest, largest):
    level, own = 1.0, jax.random.fold_in(key, 6)
    for axis_at, blocks in cuts:
        draws = jnp.exp(jax.random.uniform(jax.random.fold_in(own, axis_at), (blocks,), jnp.float32, smallest / len(cuts), largest / len(cuts)))
        level = level * jnp.repeat(draws, extent[axis_at] // blocks).reshape([-1 if axis == axis_at else 1 for axis in range(len(extent))])
    return level


def cumulative_ranks(number_of, slope):
    weights = [(1 << 20) // math.isqrt(standing ** slope) + 1 for standing in range(1, number_of + 1)]
    width = 1 + sum(weights) // (1 << 30)
    return np.cumsum(np.array([max(1, weight // width) for weight in weights]))


def skewed_ids(own_key, extent, count, skew):
    listing = cumulative_ranks(count, skew)
    lot = jax.random.randint(jax.random.fold_in(own_key, 1), extent, 0, int(listing[count - 1]))
    standing = jnp.searchsorted(jnp.asarray(listing, jnp.int32), lot, side="right")
    return jax.random.permutation(jax.random.fold_in(own_key, 2), count)[standing].astype(jnp.int32)


def centred(own_key, extent, scale, most, split=(), held_as=jnp.bfloat16):
    factor_of = level_of(own_key, extent, split, -0.22, 0.18) if split else 1.0
    array = jax.random.normal(own_key, extent, jnp.float32) * scale * factor_of
    return jnp.minimum(jnp.maximum(array, -most), most).astype(held_as)


def setup_inputs(seed: int = 0) -> dict:
    seeds = jax.random.split(jax.random.key(seed), 5)
    return {
        "ensemble": centred(seeds[0], (PARTICLES, FIELDS, LEV, NX, NY), 1.0, 6.0, ((0, 4), (3, 4), (4, 2)), jnp.float32),
        "ancestors": touch_ends(skewed_ids(seeds[1], (PARTICLES, TILES_X, TILES_Y), PARTICLES, 2), jax.random.fold_in(seeds[1], 3), 0, PARTICLES - 1).astype(jnp.int32),
        "particle_air_drag": centred(seeds[2], (PARTICLES, 2, NX, NY), 1.0, 6.0, ((0, 4), (2, 4), (3, 2)), jnp.float32),
        "eddy_diffusivity": jnp.clip(jnp.exp(jax.random.uniform(seeds[3], (LEV - 1,), jnp.float32, math.log(0.02), math.log(0.15))), 0.02, 0.15),
    }


ADVECT = 0.2
DIFFUSE = 0.15
BUOY_TEMP = 0.2
BUOY_SALT = 0.1
PRESS_SCALE = 0.25
WIND_SCALE = 0.2
CORIO_BASE = 0.1
CORIO_SLOPE = 0.1


def advance(padded, topmost_slab, eddy_diffusivity, coriolis):
    centre = padded[:, :, 1:-1, 1:-1]
    eastern_neighbour_cell = padded[:, :, 2:, 1:-1]
    west_cell = padded[:, :, :-2, 1:-1]
    north_cell = padded[:, :, 1:-1, 2:]
    south_cell = padded[:, :, 1:-1, :-2]
    grad_x = 0.5 * (eastern_neighbour_cell - west_cell)
    grad_y = 0.5 * (north_cell - south_cell)
    spread = eastern_neighbour_cell + west_cell + north_cell + south_cell - 4.0 * centre
    buoyancy = BUOY_TEMP * padded[2] - BUOY_SALT * padded[3]
    pressure = PRESS_SCALE * jnp.cumsum(buoyancy, axis=0)
    press_x = 0.5 * (pressure[:, 2:, 1:-1] - pressure[:, :-2, 1:-1])
    press_y = 0.5 * (pressure[:, 1:-1, 2:] - pressure[:, 1:-1, :-2])
    vert_flux = eddy_diffusivity[None, :, None, None] * (centre[:, 1:] - centre[:, :-1])
    closed = jnp.zeros_like(centre[:, :1])
    vertical = jnp.concatenate([vert_flux, closed], axis=1) - jnp.concatenate([closed, vert_flux], axis=1)
    east_vel = centre[0]
    north_vel = centre[1]
    carried_over = east_vel[None] * grad_x + north_vel[None] * grad_y
    common = centre - ADVECT * carried_over + DIFFUSE * spread + vertical
    level_top = (jnp.arange(centre.shape[1]) == 0).astype(jnp.float32)[:, None, None]
    forcing = WIND_SCALE * topmost_slab[:, None] * level_top
    east_next = common[0] + coriolis * north_vel - press_x + forcing[0]
    north_next = common[1] - coriolis * east_vel - press_y + forcing[1]
    return jnp.stack([east_next, north_next, common[2], common[3]])


def march_prediction(marine_variables, topmost_slab, eddy_diffusivity):
    coriolis = CORIO_BASE + CORIO_SLOPE * (jnp.arange(NY, dtype=jnp.float32) + 0.5) / NY
    for iteration in range(STEPS):
        wrapped = jnp.concatenate([marine_variables[:, :, -1:], marine_variables, marine_variables[:, :, :1]], axis=2)
        padded = jnp.pad(wrapped, ((0, 0), (0, 0), (0, 0), (1, 1)))
        marine_variables = advance(padded, topmost_slab, eddy_diffusivity, coriolis)
    return marine_variables


def reference(ensemble, ancestors, particle_air_drag, eddy_diffusivity):
    cell_source = jnp.repeat(jnp.repeat(ancestors, TILE, axis=1), TILE, axis=2)

    def per_member(particle_number):
        source_map = cell_source[particle_number].astype(jnp.int32)
        gather_idx = jnp.broadcast_to(source_map[None, None, None], (1,) + ensemble.shape[1:])
        selected_particles = jnp.take_along_axis(ensemble, gather_idx, axis=0)[0]
        return march_prediction(selected_particles, particle_air_drag[particle_number], eddy_diffusivity)

    return lax.map(per_member, jnp.arange(PARTICLES, dtype=jnp.int32))
```

```python
import functools
import math

import jax
import jax.numpy as jnp
from jax import lax
from jax.experimental import pallas as pl
from jax.experimental.pallas import tpu as pltpu
from jax.sharding import PartitionSpec as P

STEPS = 4
TILE = 8
CHUNK = 8

ADVECT = 0.2
DIFFUSE = 0.15
BUOY_TEMP = 0.2
BUOY_SALT = 0.1
PRESS_SCALE = 0.25
WIND_SCALE = 0.2
CORIO_BASE = 0.1
CORIO_SLOPE = 0.1

MESH = pl.DeviceIdType.MESH
FIELDS = 4
PAIR = 2


def remote(src, dst, send, recv, where):
    return pltpu.make_async_remote_copy(
        src_ref=src,
        dst_ref=dst,
        send_sem=send,
        recv_sem=recv,
        device_id=where,
        device_id_type=MESH,
    )


def kernel(
    slow, fast, n_gx, n_gy, ens, anc, drag, eddy, out,
    state, ag_f, ag_s, tx_f, tx_s, rx_f, rx_s, hx_out, hx_in, hy_out, hy_in,
    agf_send, agf_recv, ags_send, ags_recv, txf_send, txf_recv, txs_send, txs_recv,
    hx_send, hx_recv, hy_send, hy_recv,
):
    levels, rows, cols = ens.shape[2:]
    chunks = levels // CHUNK
    me = lax.axis_index("dom")
    a, b = me // fast, me % fast
    gx, gy = lax.axis_index("gx"), lax.axis_index("gy")
    gx_next, gx_prev = lax.rem(gx + 1, n_gx), lax.rem(gx + n_gx - 1, n_gx)
    has_left, has_right = gy > 0, gy < n_gy - 1

    def fast_peer(j):
        return a * fast + lax.rem(b + j, fast)

    def slow_peer(i):
        return lax.rem(a + i, slow) * fast + b

    barrier = pltpu.get_barrier_semaphore()
    for j in range(1, fast):
        pl.semaphore_signal(barrier, inc=1, device_id={"dom": fast_peer(j)}, device_id_type=MESH)
    for i in range(1, slow):
        pl.semaphore_signal(barrier, inc=1, device_id={"dom": slow_peer(i)}, device_id_type=MESH)
    for there in (gx_next, gx_prev):
        pl.semaphore_signal(barrier, inc=1, device_id={"gx": there}, device_id_type=MESH)

    @pl.when(has_left)
    def _():
        pl.semaphore_signal(barrier, inc=1, device_id={"gy": gy - 1}, device_id_type=MESH)

    @pl.when(has_right)
    def _():
        pl.semaphore_signal(barrier, inc=1, device_id={"gy": gy + 1}, device_id_type=MESH)

    around = has_left.astype(jnp.int32) + has_right.astype(jnp.int32)
    pl.semaphore_wait(barrier, fast - 1 + slow - 1 + 2 + around)

    def part(c):
        return pl.ds(c * CHUNK, CHUNK)

    def gather_f(j, c):
        return remote(ens.at[0, 0:PAIR, part(c)], ag_f.at[j - 1, :, part(c)],
                      agf_send.at[j - 1, c], agf_recv.at[j - 1, c], {"dom": fast_peer(j)})

    def gather_s(i, c):
        return remote(ens.at[0, PAIR:FIELDS, part(c)], ag_s.at[i - 1, :, part(c)],
                      ags_send.at[i - 1, c], ags_recv.at[i - 1, c], {"dom": slow_peer(i)})

    def onward_f(i, c):
        return remote(tx_f.at[i - 1, :, part(c)], rx_f.at[i - 1, :, part(c)],
                      txf_send.at[i - 1, c], txf_recv.at[i - 1, c], {"dom": slow_peer(i)})

    def onward_s(j, c):
        return remote(tx_s.at[j - 1, :, part(c)], rx_s.at[j - 1, :, part(c)],
                      txs_send.at[j - 1, c], txs_recv.at[j - 1, c], {"dom": fast_peer(j)})

    def row_halo(step, side, c):
        there = gx_prev if side == 0 else gx_next
        return remote(hx_out.at[step, side, c], hx_in.at[step, side, c],
                      hx_send.at[step, side, c], hx_recv.at[step, side, c], {"gx": there})

    def col_halo(step, side, c):
        there = gy + 1 if side == 0 else gy - 1
        return remote(hy_out.at[step, c], hy_in.at[step, side, c],
                      hy_send.at[step, side, c], hy_recv.at[step, side, c], {"gy": there})

    def start_halo(step, c):
        row_halo(step, 0, c).start()
        row_halo(step, 1, c).start()

        @pl.when(has_right)
        def _():
            col_halo(step, 0, c).start()

        @pl.when(has_left)
        def _():
            col_halo(step, 1, c).start()

    def wait_halo(step, c):
        row_halo(step, 0, c).wait_recv()
        row_halo(step, 1, c).wait_recv()

        @pl.when(has_left)
        def _():
            col_halo(step, 0, c).wait_recv()

        @pl.when(has_right)
        def _():
            col_halo(step, 1, c).wait_recv()

    for c in range(chunks):
        for j in range(1, fast):
            gather_f(j, c).start()
        for i in range(1, slow):
            gather_s(i, c).start()

    @pl.when(jnp.logical_not(has_left))
    def _():
        hy_in[:, 0] = jnp.zeros((STEPS, chunks, rows, cols), jnp.float32)

    @pl.when(jnp.logical_not(has_right))
    def _():
        hy_in[:, 1] = jnp.zeros((STEPS, chunks, rows, cols), jnp.float32)

    row = lax.broadcasted_iota(jnp.int32, (rows, cols), 0)
    lane = lax.broadcasted_iota(jnp.int32, (rows, cols), 1)

    def sources_of(member):
        total = jnp.zeros((rows, cols), jnp.int32)
        for tx in range(rows // TILE):
            for ty in range(cols // TILE):
                here = (lane >= ty * TILE) & (lane < (ty + 1) * TILE)
                if rows > TILE:
                    here = here & (row >= tx * TILE) & (row < (tx + 1) * TILE)
                total = jnp.where(here, anc[member, tx, ty], total)
        return total

    wanted_f = [sources_of(slow_peer(i)) for i in range(1, slow)]
    wanted_s = [sources_of(fast_peer(j)) for j in range(1, fast)]
    mine = sources_of(me)
    held_f = [a * fast + lax.rem(b + fast - j, fast) for j in range(1, fast)]
    held_s = [lax.rem(a + slow - i, slow) * fast + b for i in range(1, slow)]

    def pass_on(c, _):
        for j in range(1, fast):
            gather_f(j, c).wait_recv()
        for i in range(1, slow):
            for f in range(PAIR):
                for kk in range(CHUNK):
                    k = c * CHUNK + kk
                    value = ens[0, f, k]
                    for j in range(1, fast):
                        value = jnp.where(wanted_f[i - 1] == held_f[j - 1], ag_f[j - 1, f, k], value)
                    tx_f[i - 1, f, k] = value
            onward_f(i, c).start()
        for i in range(1, slow):
            gather_s(i, c).wait_recv()
        for j in range(1, fast):
            for f in range(PAIR):
                for kk in range(CHUNK):
                    k = c * CHUNK + kk
                    value = ens[0, PAIR + f, k]
                    for i in range(1, slow):
                        value = jnp.where(wanted_s[j - 1] == held_s[i - 1], ag_s[i - 1, f, k], value)
                    tx_s[j - 1, f, k] = value
            onward_s(j, c).start()
        return 0

    lax.fori_loop(0, chunks, pass_on, 0)

    def store_edges(step, c, f, kk, q, packed):
        hx_out[step, 0, c, f, kk : kk + 1, :] = q[0:1, :]
        hx_out[step, 1, c, f, kk : kk + 1, :] = q[rows - 1 : rows, :]
        place = 2 * (f * CHUNK + kk)
        turned = pltpu.roll(q, (place + 1) % cols, 1)
        return jnp.where((lane == place) | (lane == place + 1), turned, packed)

    blank = jnp.zeros((rows, cols), jnp.float32)
    from_f = []
    for i in range(1, slow):
        base = lax.rem(a + slow - i, slow) * fast
        from_f.append((mine >= base) & (mine < base + fast))
    from_s = []
    for j in range(1, fast):
        base = lax.rem(b + fast - j, fast)
        hit = mine == base
        for i in range(1, slow):
            hit = hit | (mine == base + i * fast)
        from_s.append(hit)

    def resample(c, _):
        for i in range(1, slow):
            onward_f(i, c).wait_recv()
        for j in range(1, fast):
            onward_s(j, c).wait_recv()
        packed = blank
        for kk in range(CHUNK):
            k = c * CHUNK + kk
            for f in range(FIELDS):
                q = ens[0, f, k]
                if f < PAIR:
                    for j in range(1, fast):
                        q = jnp.where(mine == held_f[j - 1], ag_f[j - 1, f, k], q)
                    for i in range(1, slow):
                        q = jnp.where(from_f[i - 1], rx_f[i - 1, f, k], q)
                else:
                    for i in range(1, slow):
                        q = jnp.where(mine == held_s[i - 1], ag_s[i - 1, f - PAIR, k], q)
                    for j in range(1, fast):
                        q = jnp.where(from_s[j - 1], rx_s[j - 1, f - PAIR, k], q)
                state[0, f, k] = q
                packed = store_edges(0, c, f, kk, q, packed)
        hy_out[0, c] = packed
        start_halo(0, c)
        return 0

    lax.fori_loop(0, chunks, resample, 0)

    positions = (gy * cols + lane).astype(jnp.float32)
    coriolis = CORIO_BASE + CORIO_SLOPE * (positions + 0.5) / (n_gy * cols)
    wind = (WIND_SCALE * drag[0, 0], WIND_SCALE * drag[0, 1])
    half = 0.5 * ADVECT

    for step in range(STEPS):
        now, later, final = step % 2, (step + 1) % 2, step == STEPS - 1

        def advance(c, carry, step=step, now=now, later=later, final=final):
            press_x, press_y, flux = carry
            wait_halo(step, c)
            columns = jnp.where(lane % 2 == 0, hy_in[step, 0, c], hy_in[step, 1, c])
            packed = blank
            for kk in range(CHUNK):
                k = c * CHUNK + kk
                below = jnp.minimum(k + 1, levels - 1)
                mixing = eddy[jnp.minimum(k, levels - 2)]
                u, v = state[now, 0, k], state[now, 1, k]
                c_xp, c_xm = DIFFUSE - half * u, DIFFUSE + half * u
                c_yp, c_ym = DIFFUSE - half * v, DIFFUSE + half * v
                result, new_flux, diff_x, diff_y = [], [], [], []
                for f in range(FIELDS):
                    q = state[now, f, k]
                    before = hx_in[step, 1, c, f, kk : kk + 1, :]
                    after = hx_in[step, 0, c, f, kk : kk + 1, :]
                    x_m = jnp.where(row == 0, before, pltpu.roll(q, 1, 0))
                    x_p = jnp.where(row == rows - 1, after, pltpu.roll(q, rows - 1, 0))
                    place = 2 * (f * CHUNK + kk)
                    edge = pltpu.roll(columns, cols - 1 - place, 1)
                    y_m = pltpu.roll(jnp.where(lane == cols - 1, edge, q), 1, 1)
                    y_p = pltpu.roll(jnp.where(lane == 0, edge, q), cols - 1, 1)
                    flow = mixing * (state[now, f, below] - q)
                    total = (1.0 - 4.0 * DIFFUSE) * q + (flow - flux[f])
                    total = total + (c_xp * x_p + c_xm * x_m) + (c_yp * y_p + c_ym * y_m)
                    result.append(total)
                    new_flux.append(flow)
                    if f >= PAIR:
                        diff_x.append(x_p - x_m)
                        diff_y.append(y_p - y_m)
                flux = tuple(new_flux)
                temp, salt = 0.5 * PRESS_SCALE * BUOY_TEMP, 0.5 * PRESS_SCALE * BUOY_SALT
                press_x = press_x + (temp * diff_x[0] - salt * diff_x[1])
                press_y = press_y + (temp * diff_y[0] - salt * diff_y[1])
                result[0] = result[0] + (coriolis * v - press_x)
                result[1] = result[1] - (coriolis * u + press_y)
                if kk == 0:
                    top = jnp.where(c == 0, 1.0, 0.0)
                    result[0] = result[0] + top * wind[0]
                    result[1] = result[1] + top * wind[1]
                for f in range(FIELDS):
                    if final:
                        out[0, f, k] = result[f]
                    else:
                        state[later, f, k] = result[f]
                        packed = store_edges(step + 1, c, f, kk, result[f], packed)
            if not final:
                hy_out[step + 1, c] = packed
                start_halo(step + 1, c)
            return press_x, press_y, flux

        lax.fori_loop(0, chunks, advance, (blank, blank, (blank,) * FIELDS))

    def drain(c, _):
        for j in range(1, fast):
            gather_f(j, c).wait_send()
            onward_s(j, c).wait_send()
        for i in range(1, slow):
            gather_s(i, c).wait_send()
            onward_f(i, c).wait_send()
        for step in range(STEPS):
            row_halo(step, 0, c).wait_send()
            row_halo(step, 1, c).wait_send()

            @pl.when(has_right)
            def _():
                col_halo(step, 0, c).wait_send()

            @pl.when(has_left)
            def _():
                col_halo(step, 1, c).wait_send()

        return 0

    lax.fori_loop(0, chunks, drain, 0)


def per_device(slow, fast, n_gx, n_gy, ensemble, ancestors, particle_air_drag, eddy_diffusivity):
    levels, rows, cols = ensemble.shape[2:]
    chunks = levels // CHUNK
    block = (PAIR, levels, rows, cols)
    vmem = pl.BlockSpec(memory_space=pltpu.VMEM)
    smem = pl.BlockSpec(memory_space=pltpu.SMEM)
    dma = pltpu.SemaphoreType.DMA
    f32 = jnp.float32
    return pl.pallas_call(
        functools.partial(kernel, slow, fast, n_gx, n_gy),
        out_shape=jax.ShapeDtypeStruct(ensemble.shape, f32),
        in_specs=[vmem, smem, vmem, smem],
        out_specs=vmem,
        scratch_shapes=[
            pltpu.VMEM((2, FIELDS, levels, rows, cols), f32),
            pltpu.VMEM((fast - 1,) + block, f32),
            pltpu.VMEM((slow - 1,) + block, f32),
            pltpu.VMEM((slow - 1,) + block, f32),
            pltpu.VMEM((fast - 1,) + block, f32),
            pltpu.VMEM((slow - 1,) + block, f32),
            pltpu.VMEM((fast - 1,) + block, f32),
            pltpu.VMEM((STEPS, 2, chunks, FIELDS, CHUNK, cols), f32),
            pltpu.VMEM((STEPS, 2, chunks, FIELDS, CHUNK, cols), f32),
            pltpu.VMEM((STEPS, chunks, rows, cols), f32),
            pltpu.VMEM((STEPS, 2, chunks, rows, cols), f32),
            dma((fast - 1, chunks)),
            dma((fast - 1, chunks)),
            dma((slow - 1, chunks)),
            dma((slow - 1, chunks)),
            dma((slow - 1, chunks)),
            dma((slow - 1, chunks)),
            dma((fast - 1, chunks)),
            dma((fast - 1, chunks)),
            dma((STEPS, 2, chunks)),
            dma((STEPS, 2, chunks)),
            dma((STEPS, 2, chunks)),
            dma((STEPS, 2, chunks)),
        ],
        compiler_params=pltpu.CompilerParams(
            collective_id=0, has_side_effects=True, vmem_limit_bytes=32 * 1024 * 1024
        ),
        cost_estimate=pl.CostEstimate(
            flops=STEPS * 60 * math.prod(ensemble.shape),
            bytes_accessed=8 * math.prod(ensemble.shape),
            transcendentals=0,
        ),
    )(ensemble, ancestors, particle_air_drag, eddy_diffusivity)


def solution(mesh):
    members = mesh.shape["dom"]
    fast = max(n for n in range(1, math.isqrt(members) + 1) if members % n == 0)
    placed = (
        P("dom", None, None, "gx", "gy"),
        P(None, "gx", "gy"),
        P("dom", None, "gx", "gy"),
        P(),
    )
    return jax.shard_map(
        functools.partial(
            per_device, members // fast, fast, mesh.shape["gx"], mesh.shape["gy"]
        ),
        mesh=mesh,
        in_specs=placed,
        out_specs=P("dom", None, None, "gx", "gy"),
        check_vma=False,
    )
```

```python
import functools
import math

import jax
import jax.numpy as jnp
from jax import lax
from jax.experimental import pallas as pl
from jax.experimental.pallas import tpu as pltpu
from jax.sharding import PartitionSpec as P

STEPS = 4
TILE = 8
CHUNK = 8
AHEAD = 3

ADVECT = 0.2
DIFFUSE = 0.15
BUOY_TEMP = 0.2
BUOY_SALT = 0.1
PRESS_SCALE = 0.25
WIND_SCALE = 0.2
CORIO_BASE = 0.1
CORIO_SLOPE = 0.1

MESH = pl.DeviceIdType.MESH
FIELDS = 4
PAIR = 2


def remote(src, dst, send, recv, where):
    return pltpu.make_async_remote_copy(
        src_ref=src,
        dst_ref=dst,
        send_sem=send,
        recv_sem=recv,
        device_id=where,
        device_id_type=MESH,
    )


def kernel(
    slow, fast, n_gx, n_gy, ens_hbm, anc_hbm, drag_hbm, eddy_hbm, out_hbm,
    ens, anc, drag, eddy, out, state, sums, ag_f, ag_s, tx_f, tx_s, rx_f, rx_s, hy_out, hy_in,
    local_sem, out_sem, agf_send, agf_recv, ags_send, ags_recv, txf_send, txf_recv, txs_send, txs_recv,
    hx_send, hx_recv, hy_send, hy_recv, drag_send, drag_recv,
):
    levels, rows, cols = ens.shape[2:]
    chunks = levels // CHUNK
    me = lax.axis_index("dom")
    a, b = me // fast, me % fast
    gx, gy = lax.axis_index("gx"), lax.axis_index("gy")
    gx_next, gx_prev = lax.rem(gx + 1, n_gx), lax.rem(gx + n_gx - 1, n_gx)
    has_left, has_right = gy > 0, gy < n_gy - 1

    loads = [
        pltpu.make_async_copy(there, here, local_sem.at[number])
        for number, (there, here) in enumerate(
            ((anc_hbm, anc), (ens_hbm, ens), (eddy_hbm, eddy), (drag_hbm.at[0], drag.at[0]))
        )
    ]
    for load in loads:
        load.start()

    def fast_peer(j):
        return a * fast + lax.rem(b + j, fast)

    def slow_peer(i):
        return lax.rem(a + i, slow) * fast + b

    barrier = pltpu.get_barrier_semaphore()
    for j in range(1, fast):
        pl.semaphore_signal(barrier, inc=1, device_id={"dom": fast_peer(j)}, device_id_type=MESH)
    for i in range(1, slow):
        pl.semaphore_signal(barrier, inc=1, device_id={"dom": slow_peer(i)}, device_id_type=MESH)
    for there in (gx_next, gx_prev):
        pl.semaphore_signal(barrier, inc=1, device_id={"gx": there}, device_id_type=MESH)

    @pl.when(has_left)
    def _():
        pl.semaphore_signal(barrier, inc=1, device_id={"gy": gy - 1}, device_id_type=MESH)

    @pl.when(has_right)
    def _():
        pl.semaphore_signal(barrier, inc=1, device_id={"gy": gy + 1}, device_id_type=MESH)

    around = has_left.astype(jnp.int32) + has_right.astype(jnp.int32)
    pl.semaphore_wait(barrier, fast - 1 + slow - 1 + 2 + around)

    def part(c):
        return pl.ds(c * CHUNK, CHUNK)

    def gather_f(j, c):
        return remote(ens_hbm.at[0, 0:PAIR, part(c)], ag_f.at[j - 1, :, part(c)],
                      agf_send.at[j - 1, c], agf_recv.at[j - 1, c], {"dom": fast_peer(j)})

    def gather_s(i, c):
        return remote(ens_hbm.at[0, PAIR:FIELDS, part(c)], ag_s.at[i - 1, :, part(c)],
                      ags_send.at[i - 1, c], ags_recv.at[i - 1, c], {"dom": slow_peer(i)})

    def onward_f(i, c):
        return remote(tx_f.at[i - 1, :, part(c)], rx_f.at[i - 1, :, part(c)],
                      txf_send.at[i - 1, c], txf_recv.at[i - 1, c], {"dom": slow_peer(i)})

    def onward_s(j, c):
        return remote(tx_s.at[j - 1, :, part(c)], rx_s.at[j - 1, :, part(c)],
                      txs_send.at[j - 1, c], txs_recv.at[j - 1, c], {"dom": fast_peer(j)})

    def row_halo(side, c):
        there = gx_prev if side == 0 else gx_next
        edge = slice(0, STEPS) if side == 0 else slice(rows - STEPS, rows)
        return remote(state.at[0, 0, :, part(c), edge], state.at[0, 1, :, part(c), edge],
                      hx_send.at[side, c], hx_recv.at[side, c], {"gx": there})

    def drag_halo(side):
        there = gx_prev if side == 0 else gx_next
        edge = slice(0, STEPS) if side == 0 else slice(rows - STEPS, rows)
        return remote(drag.at[0, :, edge], drag.at[1, :, edge],
                      drag_send.at[side], drag_recv.at[side], {"gx": there})

    def col_halo(step, side, c):
        there = gy + 1 if side == 0 else gy - 1
        return remote(hy_out.at[step, c], hy_in.at[step, side, c],
                      hy_send.at[step, side, c], hy_recv.at[step, side, c], {"gy": there})

    def write_out(c):
        return pltpu.make_async_copy(out.at[:, :, part(c)], out_hbm.at[:, :, part(c)], out_sem.at[c])

    def start_columns(step, c):
        @pl.when(has_right)
        def _():
            col_halo(step, 0, c).start()

        @pl.when(has_left)
        def _():
            col_halo(step, 1, c).start()

    def wait_columns(step, c):
        @pl.when(has_left)
        def _():
            col_halo(step, 0, c).wait_recv()

        @pl.when(has_right)
        def _():
            col_halo(step, 1, c).wait_recv()

    def start_gather(c):
        for j in range(1, fast):
            gather_f(j, c).start()
        for i in range(1, slow):
            gather_s(i, c).start()

    for c in range(min(AHEAD, chunks)):
        start_gather(c)

    @pl.when(jnp.logical_not(has_left))
    def _():
        hy_in[:, 0] = jnp.zeros((STEPS, chunks, rows, cols), jnp.float32)

    @pl.when(jnp.logical_not(has_right))
    def _():
        hy_in[:, 1] = jnp.zeros((STEPS, chunks, rows, cols), jnp.float32)

    sums[...] = jnp.zeros(sums.shape, jnp.float32)
    row = lax.broadcasted_iota(jnp.int32, (rows, cols), 0)
    lane = lax.broadcasted_iota(jnp.int32, (rows, cols), 1)
    loads[0].wait()

    def sources_of(member):
        total = jnp.zeros((rows, cols), jnp.int32)
        for tx in range(rows // TILE):
            for ty in range(cols // TILE):
                here = (lane >= ty * TILE) & (lane < (ty + 1) * TILE)
                if rows > TILE:
                    here = here & (row >= tx * TILE) & (row < (tx + 1) * TILE)
                total = jnp.where(here, anc[member, tx, ty], total)
        return total

    wanted_f = [sources_of(slow_peer(i)) for i in range(1, slow)]
    wanted_s = [sources_of(fast_peer(j)) for j in range(1, fast)]
    mine = sources_of(me)
    held_f = [a * fast + lax.rem(b + fast - j, fast) for j in range(1, fast)]
    held_s = [lax.rem(a + slow - i, slow) * fast + b for i in range(1, slow)]
    from_f = []
    for i in range(1, slow):
        base = lax.rem(a + slow - i, slow) * fast
        from_f.append((mine >= base) & (mine < base + fast))
    from_s = []
    for j in range(1, fast):
        base = lax.rem(b + fast - j, fast)
        hit = mine == base
        for i in range(1, slow):
            hit = hit | (mine == base + i * fast)
        from_s.append(hit)
    for load in loads[1:]:
        load.wait()
    drag_halo(0).start()
    drag_halo(1).start()

    def pass_on(c):
        for j in range(1, fast):
            gather_f(j, c).wait_recv()
        for i in range(1, slow):
            for f in range(PAIR):
                for kk in range(CHUNK):
                    k = c * CHUNK + kk
                    value = ens[0, f, k]
                    for j in range(1, fast):
                        value = jnp.where(wanted_f[i - 1] == held_f[j - 1], ag_f[j - 1, f, k], value)
                    tx_f[i - 1, f, k] = value
            onward_f(i, c).start()
        for i in range(1, slow):
            gather_s(i, c).wait_recv()
        for j in range(1, fast):
            for f in range(PAIR):
                for kk in range(CHUNK):
                    k = c * CHUNK + kk
                    value = ens[0, PAIR + f, k]
                    for i in range(1, slow):
                        value = jnp.where(wanted_s[j - 1] == held_s[i - 1], ag_s[i - 1, f, k], value)
                    tx_s[j - 1, f, k] = value
            onward_s(j, c).start()

        @pl.when(c + AHEAD < chunks)
        def _():
            start_gather(c + AHEAD)

    blank = jnp.zeros((rows, cols), jnp.float32)

    def place_of(tile, f, kk):
        return 2 * ((tile * FIELDS + f) * CHUNK + kk)

    def pack(q, place, packed):
        turned = pltpu.roll(q, (place + 1) % cols, 1)
        return jnp.where((lane == place) | (lane == place + 1), turned, packed)

    def resample(c):
        for i in range(1, slow):
            onward_f(i, c).wait_recv()
        for j in range(1, fast):
            onward_s(j, c).wait_recv()
        for kk in range(CHUNK):
            k = c * CHUNK + kk
            for f in range(FIELDS):
                q = ens[0, f, k]
                if f < PAIR:
                    for j in range(1, fast):
                        q = jnp.where(mine == held_f[j - 1], ag_f[j - 1, f, k], q)
                    for i in range(1, slow):
                        q = jnp.where(from_f[i - 1], rx_f[i - 1, f, k], q)
                else:
                    for i in range(1, slow):
                        q = jnp.where(mine == held_s[i - 1], ag_s[i - 1, f - PAIR, k], q)
                    for j in range(1, fast):
                        q = jnp.where(from_s[j - 1], rx_s[j - 1, f - PAIR, k], q)
                state[0, 0, f, k] = q
        row_halo(0, c).start()
        row_halo(1, c).start()

    def first_columns(c):
        row_halo(0, c).wait_recv()
        row_halo(1, c).wait_recv()
        packed = blank
        for tile in range(2):
            for f in range(FIELDS):
                for kk in range(CHUNK):
                    packed = pack(state[0, tile, f, c * CHUNK + kk], place_of(tile, f, kk), packed)
        hy_out[0, c] = packed
        start_columns(0, c)

    positions = (gy * cols + lane).astype(jnp.float32)
    coriolis = CORIO_BASE + CORIO_SLOPE * (positions + 0.5) / (n_gy * cols)
    half = 0.5 * ADVECT
    temp, salt = 0.5 * PRESS_SCALE * BUOY_TEMP, 0.5 * PRESS_SCALE * BUOY_SALT

    def advance(step, c, final):
        tiles = (0,) if final else (0, 1)
        wait_columns(step, c)
        columns = jnp.where(lane % 2 == 0, hy_in[step, 0, c], hy_in[step, 1, c])
        packed = blank
        press_x = [sums[step, t, 0] for t in tiles]
        press_y = [sums[step, t, 1] for t in tiles]
        flux = [[sums[step, t, 2 + f] for f in range(FIELDS)] for t in tiles]
        for kk in range(CHUNK):
            k = c * CHUNK + kk
            below = jnp.minimum(k + 1, levels - 1)
            mixing = eddy[jnp.minimum(k, levels - 2)]
            now = [[state[step, t, f, k] for f in range(FIELDS)] for t in (0, 1)]
            result = [[None] * FIELDS for t in tiles]
            coef = []
            for t in tiles:
                u, v = now[t][0], now[t][1]
                coef.append((DIFFUSE + half * u, DIFFUSE - half * u, DIFFUSE + half * v, DIFFUSE - half * v))
            diff_x, diff_y = [[] for t in tiles], [[] for t in tiles]
            for f in range(FIELDS):
                up = [pltpu.roll(now[t][f], 1, 0) for t in (0, 1)]
                down = [pltpu.roll(now[t][f], rows - 1, 0) for t in (0, 1)]
                for t in tiles:
                    q = now[t][f]
                    x_m = jnp.where(row == 0, up[1 - t], up[t])
                    x_p = jnp.where(row == rows - 1, down[1 - t], down[t])
                    edge = pltpu.roll(columns, cols - 1 - place_of(t, f, kk), 1)
                    y_m = pltpu.roll(jnp.where(lane == cols - 1, edge, q), 1, 1)
                    y_p = pltpu.roll(jnp.where(lane == 0, edge, q), cols - 1, 1)
                    flow = mixing * (state[step, t, f, below] - q)
                    total = (1.0 - 4.0 * DIFFUSE) * q + (flow - flux[t][f])
                    c_xm, c_xp, c_ym, c_yp = coef[t]
                    total = total + (c_xp * x_p + c_xm * x_m) + (c_yp * y_p + c_ym * y_m)
                    result[t][f] = total
                    flux[t][f] = flow
                    if f >= PAIR:
                        diff_x[t].append(x_p - x_m)
                        diff_y[t].append(y_p - y_m)
            for t in tiles:
                press_x[t] = press_x[t] + (temp * diff_x[t][0] - salt * diff_x[t][1])
                press_y[t] = press_y[t] + (temp * diff_y[t][0] - salt * diff_y[t][1])
                result[t][0] = result[t][0] + (coriolis * now[t][1] - press_x[t])
                result[t][1] = result[t][1] - (coriolis * now[t][0] + press_y[t])
                if kk == 0:
                    top = jnp.where(c == 0, WIND_SCALE, 0.0)
                    result[t][0] = result[t][0] + top * drag[t, 0]
                    result[t][1] = result[t][1] + top * drag[t, 1]
                for f in range(FIELDS):
                    if final:
                        out[0, f, k] = result[t][f]
                    else:
                        state[step + 1, t, f, k] = result[t][f]
                        packed = pack(result[t][f], place_of(t, f, kk), packed)
        for t in tiles:
            sums[step, t, 0] = press_x[t]
            sums[step, t, 1] = press_y[t]
            for f in range(FIELDS):
                sums[step, t, 2 + f] = flux[t][f]
        if final:
            write_out(c).start()
        else:
            hy_out[step + 1, c] = packed
            start_columns(step + 1, c)

    drag_halo(0).wait_recv()
    drag_halo(1).wait_recv()

    def tick(t, _):
        def at(c, body):
            @pl.when((c >= 0) & (c < chunks))
            def _():
                body(c)

        at(t, pass_on)
        at(t - 1, resample)
        at(t - 2, first_columns)

        def one(step, _):
            at(t - 3 - step, lambda c: advance(step, c, False))
            return 0

        lax.fori_loop(0, STEPS - 1, one, 0)
        at(t - 2 - STEPS, lambda c: advance(STEPS - 1, c, True))
        return 0

    lax.fori_loop(0, chunks + STEPS + 2, tick, 0)

    def drain(c, _):
        for j in range(1, fast):
            gather_f(j, c).wait_send()
            onward_s(j, c).wait_send()
        for i in range(1, slow):
            gather_s(i, c).wait_send()
            onward_f(i, c).wait_send()
        row_halo(0, c).wait_send()
        row_halo(1, c).wait_send()
        write_out(c).wait()
        for step in range(STEPS):
            @pl.when(has_right)
            def _():
                col_halo(step, 0, c).wait_send()

            @pl.when(has_left)
            def _():
                col_halo(step, 1, c).wait_send()

        return 0

    lax.fori_loop(0, chunks, drain, 0)
    drag_halo(0).wait_send()
    drag_halo(1).wait_send()


def per_device(slow, fast, n_gx, n_gy, ensemble, ancestors, particle_air_drag, eddy_diffusivity):
    levels, rows, cols = ensemble.shape[2:]
    chunks = levels // CHUNK
    block = (PAIR, levels, rows, cols)
    hbm = pl.BlockSpec(memory_space=pltpu.HBM)
    dma = pltpu.SemaphoreType.DMA
    f32 = jnp.float32
    return pl.pallas_call(
        functools.partial(kernel, slow, fast, n_gx, n_gy),
        out_shape=jax.ShapeDtypeStruct(ensemble.shape, f32),
        in_specs=[hbm] * 4,
        out_specs=hbm,
        scratch_shapes=[
            pltpu.VMEM(ensemble.shape, f32),
            pltpu.SMEM(ancestors.shape, jnp.int32),
            pltpu.VMEM((2,) + particle_air_drag.shape[1:], f32),
            pltpu.SMEM(eddy_diffusivity.shape, f32),
            pltpu.VMEM(ensemble.shape, f32),
            pltpu.VMEM((STEPS, 2, FIELDS, levels, rows, cols), f32),
            pltpu.VMEM((STEPS, 2, 2 + FIELDS, rows, cols), f32),
            pltpu.VMEM((fast - 1,) + block, f32),
            pltpu.VMEM((slow - 1,) + block, f32),
            pltpu.VMEM((slow - 1,) + block, f32),
            pltpu.VMEM((fast - 1,) + block, f32),
            pltpu.VMEM((slow - 1,) + block, f32),
            pltpu.VMEM((fast - 1,) + block, f32),
            pltpu.VMEM((STEPS, chunks, rows, cols), f32),
            pltpu.VMEM((STEPS, 2, chunks, rows, cols), f32),
            dma((4,)),
            dma((chunks,)),
            dma((fast - 1, chunks)),
            dma((fast - 1, chunks)),
            dma((slow - 1, chunks)),
            dma((slow - 1, chunks)),
            dma((slow - 1, chunks)),
            dma((slow - 1, chunks)),
            dma((fast - 1, chunks)),
            dma((fast - 1, chunks)),
            dma((2, chunks)),
            dma((2, chunks)),
            dma((STEPS, 2, chunks)),
            dma((STEPS, 2, chunks)),
            dma((2,)),
            dma((2,)),
        ],
        compiler_params=pltpu.CompilerParams(
            collective_id=0, has_side_effects=True, vmem_limit_bytes=32 * 1024 * 1024
        ),
        cost_estimate=pl.CostEstimate(
            flops=STEPS * 60 * math.prod(ensemble.shape),
            bytes_accessed=8 * math.prod(ensemble.shape),
            transcendentals=0,
        ),
    )(ensemble, ancestors, particle_air_drag, eddy_diffusivity)


def solution(mesh):
    members = mesh.shape["dom"]
    fast = max(n for n in range(1, math.isqrt(members) + 1) if members % n == 0)
    placed = (
        P("dom", None, None, "gx", "gy"),
        P(None, "gx", "gy"),
        P("dom", None, "gx", "gy"),
        P(),
    )
    return jax.shard_map(
        functools.partial(
            per_device, members // fast, fast, mesh.shape["gx"], mesh.shape["gy"]
        ),
        mesh=mesh,
        in_specs=placed,
        out_specs=P("dom", None, None, "gx", "gy"),
        check_vma=False,
    )
```

```python
import functools
import math

import jax
import jax.numpy as jnp
from jax import lax
from jax.experimental import pallas as pl
from jax.experimental.pallas import tpu as pltpu
from jax.sharding import PartitionSpec as P

STEPS = 4
TILE = 8
CHUNK = 8
AHEAD = 3

ADVECT = 0.2
DIFFUSE = 0.15
BUOY_TEMP = 0.2
BUOY_SALT = 0.1
PRESS_SCALE = 0.25
WIND_SCALE = 0.2
CORIO_BASE = 0.1
CORIO_SLOPE = 0.1

MESH = pl.DeviceIdType.MESH
FIELDS = 4
PAIR = 2


def remote(src, dst, send, recv, where):
    return pltpu.make_async_remote_copy(
        src_ref=src,
        dst_ref=dst,
        send_sem=send,
        recv_sem=recv,
        device_id=where,
        device_id_type=MESH,
    )


def kernel(
    slow, fast, n_gx, n_gy, ens_hbm, anc_hbm, drag_hbm, eddy_hbm, out_hbm,
    ens, anc, drag, eddy, out, state, sums, ag_f, ag_s, tx_f, tx_s, rx_f, rx_s, hy_out, hy_in,
    local_sem, out_sem, agf_send, agf_recv, ags_send, ags_recv, txf_send, txf_recv, txs_send, txs_recv,
    hx_send, hx_recv, hy_send, hy_recv, drag_send, drag_recv,
):
    levels, rows, cols = ens.shape[2:]
    chunks = levels // CHUNK
    me = lax.axis_index("dom")
    a, b = me // fast, me % fast
    gx, gy = lax.axis_index("gx"), lax.axis_index("gy")
    gx_next, gx_prev = lax.rem(gx + 1, n_gx), lax.rem(gx + n_gx - 1, n_gx)
    has_left, has_right = gy > 0, gy < n_gy - 1

    loads = [
        pltpu.make_async_copy(there, here, local_sem.at[number])
        for number, (there, here) in enumerate(
            ((anc_hbm, anc), (ens_hbm, ens), (eddy_hbm, eddy), (drag_hbm.at[0], drag.at[0]))
        )
    ]
    for load in loads:
        load.start()

    def fast_peer(j):
        return a * fast + lax.rem(b + j, fast)

    def slow_peer(i):
        return lax.rem(a + i, slow) * fast + b

    barrier = pltpu.get_barrier_semaphore()
    for j in range(1, fast):
        pl.semaphore_signal(barrier, inc=1, device_id={"dom": fast_peer(j)}, device_id_type=MESH)
    for i in range(1, slow):
        pl.semaphore_signal(barrier, inc=1, device_id={"dom": slow_peer(i)}, device_id_type=MESH)
    for there in (gx_next, gx_prev):
        pl.semaphore_signal(barrier, inc=1, device_id={"gx": there}, device_id_type=MESH)

    @pl.when(has_left)
    def _():
        pl.semaphore_signal(barrier, inc=1, device_id={"gy": gy - 1}, device_id_type=MESH)

    @pl.when(has_right)
    def _():
        pl.semaphore_signal(barrier, inc=1, device_id={"gy": gy + 1}, device_id_type=MESH)

    around = has_left.astype(jnp.int32) + has_right.astype(jnp.int32)
    pl.semaphore_wait(barrier, fast - 1 + slow - 1 + 2 + around)

    def part(c):
        return pl.ds(c * CHUNK, CHUNK)

    def gather_f(j, c):
        return remote(ens_hbm.at[0, 0:PAIR, part(c)], ag_f.at[j - 1, :, part(c)],
                      agf_send.at[j - 1, c], agf_recv.at[j - 1, c], {"dom": fast_peer(j)})

    def gather_s(i, c):
        return remote(ens_hbm.at[0, PAIR:FIELDS, part(c)], ag_s.at[i - 1, :, part(c)],
                      ags_send.at[i - 1, c], ags_recv.at[i - 1, c], {"dom": slow_peer(i)})

    def onward_f(i, c):
        return remote(tx_f.at[i - 1, :, part(c)], rx_f.at[i - 1, :, part(c)],
                      txf_send.at[i - 1, c], txf_recv.at[i - 1, c], {"dom": slow_peer(i)})

    def onward_s(j, c):
        return remote(tx_s.at[j - 1, :, part(c)], rx_s.at[j - 1, :, part(c)],
                      txs_send.at[j - 1, c], txs_recv.at[j - 1, c], {"dom": fast_peer(j)})

    def row_halo(side, c):
        there = gx_prev if side == 0 else gx_next
        edge = slice(0, STEPS) if side == 0 else slice(rows - STEPS, rows)
        return remote(state.at[0, 0, :, part(c), edge], state.at[0, 1, :, part(c), edge],
                      hx_send.at[side, c], hx_recv.at[side, c], {"gx": there})

    def drag_halo(side):
        there = gx_prev if side == 0 else gx_next
        edge = slice(0, STEPS) if side == 0 else slice(rows - STEPS, rows)
        return remote(drag.at[0, :, edge], drag.at[1, :, edge],
                      drag_send.at[side], drag_recv.at[side], {"gx": there})

    def col_halo(step, side, c):
        there = gy + 1 if side == 0 else gy - 1
        return remote(hy_out.at[step, c], hy_in.at[step, side, c],
                      hy_send.at[step, side, c], hy_recv.at[step, side, c], {"gy": there})

    def write_out(c):
        return pltpu.make_async_copy(out.at[:, :, part(c)], out_hbm.at[:, :, part(c)], out_sem.at[c])

    def start_columns(step, c):
        @pl.when(has_right)
        def _():
            col_halo(step, 0, c).start()

        @pl.when(has_left)
        def _():
            col_halo(step, 1, c).start()

    def wait_columns(step, c):
        @pl.when(has_left)
        def _():
            col_halo(step, 0, c).wait_recv()

        @pl.when(has_right)
        def _():
            col_halo(step, 1, c).wait_recv()

    def start_gather(c):
        for j in range(1, fast):
            gather_f(j, c).start()
        for i in range(1, slow):
            gather_s(i, c).start()

    for c in range(min(AHEAD, chunks)):
        start_gather(c)

    @pl.when(jnp.logical_not(has_left))
    def _():
        hy_in[:, 0] = jnp.zeros((STEPS, chunks, rows, cols), jnp.float32)

    @pl.when(jnp.logical_not(has_right))
    def _():
        hy_in[:, 1] = jnp.zeros((STEPS, chunks, rows, cols), jnp.float32)

    sums[...] = jnp.zeros(sums.shape, jnp.float32)
    row = lax.broadcasted_iota(jnp.int32, (rows, cols), 0)
    lane = lax.broadcasted_iota(jnp.int32, (rows, cols), 1)
    loads[0].wait()

    def sources_of(member):
        total = jnp.zeros((rows, cols), jnp.int32)
        for tx in range(rows // TILE):
            for ty in range(cols // TILE):
                here = (lane >= ty * TILE) & (lane < (ty + 1) * TILE)
                if rows > TILE:
                    here = here & (row >= tx * TILE) & (row < (tx + 1) * TILE)
                total = jnp.where(here, anc[member, tx, ty], total)
        return total

    wanted_f = [sources_of(slow_peer(i)) for i in range(1, slow)]
    wanted_s = [sources_of(fast_peer(j)) for j in range(1, fast)]
    mine = sources_of(me)
    held_f = [a * fast + lax.rem(b + fast - j, fast) for j in range(1, fast)]
    held_s = [lax.rem(a + slow - i, slow) * fast + b for i in range(1, slow)]
    from_f = []
    for i in range(1, slow):
        base = lax.rem(a + slow - i, slow) * fast
        from_f.append((mine >= base) & (mine < base + fast))
    from_s = []
    for j in range(1, fast):
        base = lax.rem(b + fast - j, fast)
        hit = mine == base
        for i in range(1, slow):
            hit = hit | (mine == base + i * fast)
        from_s.append(hit)
    for load in loads[1:]:
        load.wait()
    drag_halo(0).start()
    drag_halo(1).start()

    def pass_on(c):
        for j in range(1, fast):
            gather_f(j, c).wait_recv()
        for i in range(1, slow):
            chosen = []
            for f in range(PAIR):
                for kk in range(CHUNK):
                    k = c * CHUNK + kk
                    value = ens[0, f, k]
                    for j in range(1, fast):
                        value = jnp.where(wanted_f[i - 1] == held_f[j - 1], ag_f[j - 1, f, k], value)
                    chosen.append((f, k, value))
            for f, k, value in chosen:
                tx_f[i - 1, f, k] = value
            onward_f(i, c).start()
        for i in range(1, slow):
            gather_s(i, c).wait_recv()
        for j in range(1, fast):
            chosen = []
            for f in range(PAIR):
                for kk in range(CHUNK):
                    k = c * CHUNK + kk
                    value = ens[0, PAIR + f, k]
                    for i in range(1, slow):
                        value = jnp.where(wanted_s[j - 1] == held_s[i - 1], ag_s[i - 1, f, k], value)
                    chosen.append((f, k, value))
            for f, k, value in chosen:
                tx_s[j - 1, f, k] = value
            onward_s(j, c).start()

        @pl.when(c + AHEAD < chunks)
        def _():
            start_gather(c + AHEAD)

    blank = jnp.zeros((rows, cols), jnp.float32)

    def place_of(tile, f, kk):
        return 2 * ((tile * FIELDS + f) * CHUNK + kk)

    def pack(q, place, packed):
        turned = pltpu.roll(q, (place + 1) % cols, 1)
        return jnp.where((lane == place) | (lane == place + 1), turned, packed)

    def resample(c):
        for i in range(1, slow):
            onward_f(i, c).wait_recv()
        for j in range(1, fast):
            onward_s(j, c).wait_recv()
        chosen = []
        for kk in range(CHUNK):
            k = c * CHUNK + kk
            for f in range(FIELDS):
                q = ens[0, f, k]
                if f < PAIR:
                    for j in range(1, fast):
                        q = jnp.where(mine == held_f[j - 1], ag_f[j - 1, f, k], q)
                    for i in range(1, slow):
                        q = jnp.where(from_f[i - 1], rx_f[i - 1, f, k], q)
                else:
                    for i in range(1, slow):
                        q = jnp.where(mine == held_s[i - 1], ag_s[i - 1, f - PAIR, k], q)
                    for j in range(1, fast):
                        q = jnp.where(from_s[j - 1], rx_s[j - 1, f - PAIR, k], q)
                chosen.append((f, k, q))
        for f, k, q in chosen:
            state[0, 0, f, k] = q
        row_halo(0, c).start()
        row_halo(1, c).start()

    def first_columns(c):
        row_halo(0, c).wait_recv()
        row_halo(1, c).wait_recv()
        packed = blank
        for tile in range(2):
            for f in range(FIELDS):
                for kk in range(CHUNK):
                    packed = pack(state[0, tile, f, c * CHUNK + kk], place_of(tile, f, kk), packed)
        hy_out[0, c] = packed
        start_columns(0, c)

    positions = (gy * cols + lane).astype(jnp.float32)
    coriolis = CORIO_BASE + CORIO_SLOPE * (positions + 0.5) / (n_gy * cols)
    half = 0.5 * ADVECT
    temp, salt = 0.5 * PRESS_SCALE * BUOY_TEMP, 0.5 * PRESS_SCALE * BUOY_SALT

    def advance(step, c, final):
        tiles = (0,) if final else (0, 1)
        wait_columns(step, c)
        columns = jnp.where(lane % 2 == 0, hy_in[step, 0, c], hy_in[step, 1, c])
        packed = blank
        press_x = [sums[step, t, 0] for t in tiles]
        press_y = [sums[step, t, 1] for t in tiles]
        flux = [[sums[step, t, 2 + f] for f in range(FIELDS)] for t in tiles]
        finished = []
        for kk in range(CHUNK):
            k = c * CHUNK + kk
            below = jnp.minimum(k + 1, levels - 1)
            mixing = eddy[jnp.minimum(k, levels - 2)]
            now = [[state[step, t, f, k] for f in range(FIELDS)] for t in (0, 1)]
            result = [[None] * FIELDS for t in tiles]
            coef = []
            for t in tiles:
                u, v = now[t][0], now[t][1]
                coef.append((DIFFUSE + half * u, DIFFUSE - half * u, DIFFUSE + half * v, DIFFUSE - half * v))
            diff_x, diff_y = [[] for t in tiles], [[] for t in tiles]
            for f in range(FIELDS):
                up = [pltpu.roll(now[t][f], 1, 0) for t in (0, 1)]
                down = [pltpu.roll(now[t][f], rows - 1, 0) for t in (0, 1)]
                for t in tiles:
                    q = now[t][f]
                    x_m = jnp.where(row == 0, up[1 - t], up[t])
                    x_p = jnp.where(row == rows - 1, down[1 - t], down[t])
                    edge = pltpu.roll(columns, cols - 1 - place_of(t, f, kk), 1)
                    y_m = pltpu.roll(jnp.where(lane == cols - 1, edge, q), 1, 1)
                    y_p = pltpu.roll(jnp.where(lane == 0, edge, q), cols - 1, 1)
                    flow = mixing * (state[step, t, f, below] - q)
                    total = (1.0 - 4.0 * DIFFUSE) * q + (flow - flux[t][f])
                    c_xm, c_xp, c_ym, c_yp = coef[t]
                    total = total + (c_xp * x_p + c_xm * x_m) + (c_yp * y_p + c_ym * y_m)
                    result[t][f] = total
                    flux[t][f] = flow
                    if f >= PAIR:
                        diff_x[t].append(x_p - x_m)
                        diff_y[t].append(y_p - y_m)
            for t in tiles:
                press_x[t] = press_x[t] + (temp * diff_x[t][0] - salt * diff_x[t][1])
                press_y[t] = press_y[t] + (temp * diff_y[t][0] - salt * diff_y[t][1])
                result[t][0] = result[t][0] + (coriolis * now[t][1] - press_x[t])
                result[t][1] = result[t][1] - (coriolis * now[t][0] + press_y[t])
                if kk == 0:
                    top = jnp.where(c == 0, WIND_SCALE, 0.0)
                    result[t][0] = result[t][0] + top * drag[t, 0]
                    result[t][1] = result[t][1] + top * drag[t, 1]
                for f in range(FIELDS):
                    finished.append((t, f, k, result[t][f]))
                    if not final:
                        packed = pack(result[t][f], place_of(t, f, kk), packed)
        for t, f, k, value in finished:
            if final:
                out[0, f, k] = value
            else:
                state[step + 1, t, f, k] = value
        for t in tiles:
            sums[step, t, 0] = press_x[t]
            sums[step, t, 1] = press_y[t]
            for f in range(FIELDS):
                sums[step, t, 2 + f] = flux[t][f]
        if final:
            write_out(c).start()
        else:
            hy_out[step + 1, c] = packed
            start_columns(step + 1, c)

    drag_halo(0).wait_recv()
    drag_halo(1).wait_recv()

    def tick(t, _):
        def at(c, body):
            @pl.when((c >= 0) & (c < chunks))
            def _():
                body(c)

        at(t, pass_on)
        at(t - 1, resample)
        at(t - 2, first_columns)

        def one(step, _):
            at(t - 3 - step, lambda c: advance(step, c, False))
            return 0

        lax.fori_loop(0, STEPS - 1, one, 0)
        at(t - 2 - STEPS, lambda c: advance(STEPS - 1, c, True))
        return 0

    lax.fori_loop(0, chunks + STEPS + 2, tick, 0)

    def drain(c, _):
        for j in range(1, fast):
            gather_f(j, c).wait_send()
            onward_s(j, c).wait_send()
        for i in range(1, slow):
            gather_s(i, c).wait_send()
            onward_f(i, c).wait_send()
        row_halo(0, c).wait_send()
        row_halo(1, c).wait_send()
        write_out(c).wait()
        for step in range(STEPS):
            @pl.when(has_right)
            def _():
                col_halo(step, 0, c).wait_send()

            @pl.when(has_left)
            def _():
                col_halo(step, 1, c).wait_send()

        return 0

    lax.fori_loop(0, chunks, drain, 0)
    drag_halo(0).wait_send()
    drag_halo(1).wait_send()


def per_device(slow, fast, n_gx, n_gy, ensemble, ancestors, particle_air_drag, eddy_diffusivity):
    levels, rows, cols = ensemble.shape[2:]
    chunks = levels // CHUNK
    block = (PAIR, levels, rows, cols)
    hbm = pl.BlockSpec(memory_space=pltpu.HBM)
    dma = pltpu.SemaphoreType.DMA
    f32 = jnp.float32
    return pl.pallas_call(
        functools.partial(kernel, slow, fast, n_gx, n_gy),
        out_shape=jax.ShapeDtypeStruct(ensemble.shape, f32),
        in_specs=[hbm] * 4,
        out_specs=hbm,
        scratch_shapes=[
            pltpu.VMEM(ensemble.shape, f32),
            pltpu.SMEM(ancestors.shape, jnp.int32),
            pltpu.VMEM((2,) + particle_air_drag.shape[1:], f32),
            pltpu.SMEM(eddy_diffusivity.shape, f32),
            pltpu.VMEM(ensemble.shape, f32),
            pltpu.VMEM((STEPS, 2, FIELDS, levels, rows, cols), f32),
            pltpu.VMEM((STEPS, 2, 2 + FIELDS, rows, cols), f32),
            pltpu.VMEM((fast - 1,) + block, f32),
            pltpu.VMEM((slow - 1,) + block, f32),
            pltpu.VMEM((slow - 1,) + block, f32),
            pltpu.VMEM((fast - 1,) + block, f32),
            pltpu.VMEM((slow - 1,) + block, f32),
            pltpu.VMEM((fast - 1,) + block, f32),
            pltpu.VMEM((STEPS, chunks, rows, cols), f32),
            pltpu.VMEM((STEPS, 2, chunks, rows, cols), f32),
            dma((4,)),
            dma((chunks,)),
            dma((fast - 1, chunks)),
            dma((fast - 1, chunks)),
            dma((slow - 1, chunks)),
            dma((slow - 1, chunks)),
            dma((slow - 1, chunks)),
            dma((slow - 1, chunks)),
            dma((fast - 1, chunks)),
            dma((fast - 1, chunks)),
            dma((2, chunks)),
            dma((2, chunks)),
            dma((STEPS, 2, chunks)),
            dma((STEPS, 2, chunks)),
            dma((2,)),
            dma((2,)),
        ],
        compiler_params=pltpu.CompilerParams(
            collective_id=0, has_side_effects=True, vmem_limit_bytes=64 * 1024 * 1024
        ),
        cost_estimate=pl.CostEstimate(
            flops=STEPS * 60 * math.prod(ensemble.shape),
            bytes_accessed=8 * math.prod(ensemble.shape),
            transcendentals=0,
        ),
    )(ensemble, ancestors, particle_air_drag, eddy_diffusivity)


def solution(mesh):
    members = mesh.shape["dom"]
    fast = max(n for n in range(1, math.isqrt(members) + 1) if members % n == 0)
    placed = (
        P("dom", None, None, "gx", "gy"),
        P(None, "gx", "gy"),
        P("dom", None, "gx", "gy"),
        P(),
    )
    return jax.shard_map(
        functools.partial(
            per_device, members // fast, fast, mesh.shape["gx"], mesh.shape["gy"]
        ),
        mesh=mesh,
        in_specs=placed,
        out_specs=P("dom", None, None, "gx", "gy"),
        check_vma=False,
    )
```

```python
import functools
import math

import jax
import jax.numpy as jnp
from jax import lax
from jax.experimental import pallas as pl
from jax.experimental.pallas import tpu as pltpu
from jax.sharding import PartitionSpec as P

STEPS = 4
TILE = 8
CHUNK = 4
AHEAD = 3

ADVECT = 0.2
DIFFUSE = 0.15
BUOY_TEMP = 0.2
BUOY_SALT = 0.1
PRESS_SCALE = 0.25
WIND_SCALE = 0.2
CORIO_BASE = 0.1
CORIO_SLOPE = 0.1

MESH = pl.DeviceIdType.MESH
FIELDS = 4
PAIR = 2


def remote(src, dst, send, recv, where):
    return pltpu.make_async_remote_copy(
        src_ref=src,
        dst_ref=dst,
        send_sem=send,
        recv_sem=recv,
        device_id=where,
        device_id_type=MESH,
    )


def kernel(
    slow, fast, n_gx, n_gy, ens_hbm, anc_hbm, drag_hbm, eddy_hbm, out_hbm,
    ens, anc, drag, eddy, out, state_0, state_1, state_2, state_3, sums, ag_f, ag_s, tx_f, tx_s, rx_f, rx_s, hy_out, hy_in,
    local_sem, out_sem, agf_send, agf_recv, ags_send, ags_recv, txf_send, txf_recv, txs_send, txs_recv,
    hx_send, hx_recv, hy_send, hy_recv, drag_send, drag_recv,
):
    levels, rows, cols = ens.shape[2:]
    chunks = levels // CHUNK
    states = (state_0, state_1, state_2, state_3)
    me = lax.axis_index("dom")
    a, b = me // fast, me % fast
    gx, gy = lax.axis_index("gx"), lax.axis_index("gy")
    gx_next, gx_prev = lax.rem(gx + 1, n_gx), lax.rem(gx + n_gx - 1, n_gx)
    has_left, has_right = gy > 0, gy < n_gy - 1

    loads = [
        pltpu.make_async_copy(there, here, local_sem.at[number])
        for number, (there, here) in enumerate(
            ((anc_hbm, anc), (ens_hbm, ens), (eddy_hbm, eddy), (drag_hbm.at[0], drag.at[0]))
        )
    ]
    for load in loads:
        load.start()

    def fast_peer(j):
        return a * fast + lax.rem(b + j, fast)

    def slow_peer(i):
        return lax.rem(a + i, slow) * fast + b

    barrier = pltpu.get_barrier_semaphore()
    for j in range(1, fast):
        pl.semaphore_signal(barrier, inc=1, device_id={"dom": fast_peer(j)}, device_id_type=MESH)
    for i in range(1, slow):
        pl.semaphore_signal(barrier, inc=1, device_id={"dom": slow_peer(i)}, device_id_type=MESH)
    for there in (gx_next, gx_prev):
        pl.semaphore_signal(barrier, inc=1, device_id={"gx": there}, device_id_type=MESH)

    @pl.when(has_left)
    def _():
        pl.semaphore_signal(barrier, inc=1, device_id={"gy": gy - 1}, device_id_type=MESH)

    @pl.when(has_right)
    def _():
        pl.semaphore_signal(barrier, inc=1, device_id={"gy": gy + 1}, device_id_type=MESH)

    around = has_left.astype(jnp.int32) + has_right.astype(jnp.int32)
    pl.semaphore_wait(barrier, fast - 1 + slow - 1 + 2 + around)

    def part(c):
        return pl.ds(c * CHUNK, CHUNK)

    def gather_f(j, c):
        return remote(ens_hbm.at[0, 0:PAIR, part(c)], ag_f.at[j - 1, :, part(c)],
                      agf_send.at[j - 1, c], agf_recv.at[j - 1, c], {"dom": fast_peer(j)})

    def gather_s(i, c):
        return remote(ens_hbm.at[0, PAIR:FIELDS, part(c)], ag_s.at[i - 1, :, part(c)],
                      ags_send.at[i - 1, c], ags_recv.at[i - 1, c], {"dom": slow_peer(i)})

    def onward_f(i, c):
        return remote(tx_f.at[i - 1, :, part(c)], rx_f.at[i - 1, :, part(c)],
                      txf_send.at[i - 1, c], txf_recv.at[i - 1, c], {"dom": slow_peer(i)})

    def onward_s(j, c):
        return remote(tx_s.at[j - 1, :, part(c)], rx_s.at[j - 1, :, part(c)],
                      txs_send.at[j - 1, c], txs_recv.at[j - 1, c], {"dom": fast_peer(j)})

    def row_halo(side, c):
        there = gx_prev if side == 0 else gx_next
        edge = slice(0, STEPS) if side == 0 else slice(rows - STEPS, rows)
        return remote(state_0.at[0, :, part(c), edge], state_0.at[1, :, part(c), edge],
                      hx_send.at[side, c], hx_recv.at[side, c], {"gx": there})

    def drag_halo(side):
        there = gx_prev if side == 0 else gx_next
        edge = slice(0, STEPS) if side == 0 else slice(rows - STEPS, rows)
        return remote(drag.at[0, :, edge], drag.at[1, :, edge],
                      drag_send.at[side], drag_recv.at[side], {"gx": there})

    def col_halo(step, side, c):
        there = gy + 1 if side == 0 else gy - 1
        return remote(hy_out.at[step, c], hy_in.at[step, side, c],
                      hy_send.at[step, side, c], hy_recv.at[step, side, c], {"gy": there})

    def write_out(c):
        return pltpu.make_async_copy(out.at[:, :, part(c)], out_hbm.at[:, :, part(c)], out_sem.at[c])

    def start_columns(step, c):
        @pl.when(has_right)
        def _():
            col_halo(step, 0, c).start()

        @pl.when(has_left)
        def _():
            col_halo(step, 1, c).start()

    def wait_columns(step, c):
        @pl.when(has_left)
        def _():
            col_halo(step, 0, c).wait_recv()

        @pl.when(has_right)
        def _():
            col_halo(step, 1, c).wait_recv()

    def start_gather(c):
        for j in range(1, fast):
            gather_f(j, c).start()
        for i in range(1, slow):
            gather_s(i, c).start()

    for c in range(min(AHEAD, chunks)):
        start_gather(c)

    @pl.when(jnp.logical_not(has_left))
    def _():
        hy_in[:, 0] = jnp.zeros((STEPS, chunks, rows, cols), jnp.float32)

    @pl.when(jnp.logical_not(has_right))
    def _():
        hy_in[:, 1] = jnp.zeros((STEPS, chunks, rows, cols), jnp.float32)

    sums[...] = jnp.zeros(sums.shape, jnp.float32)
    row = lax.broadcasted_iota(jnp.int32, (rows, cols), 0)
    lane = lax.broadcasted_iota(jnp.int32, (rows, cols), 1)
    loads[0].wait()

    def sources_of(member):
        total = jnp.zeros((rows, cols), jnp.int32)
        for tx in range(rows // TILE):
            for ty in range(cols // TILE):
                here = (lane >= ty * TILE) & (lane < (ty + 1) * TILE)
                if rows > TILE:
                    here = here & (row >= tx * TILE) & (row < (tx + 1) * TILE)
                total = jnp.where(here, anc[member, tx, ty], total)
        return total

    wanted_f = [sources_of(slow_peer(i)) for i in range(1, slow)]
    wanted_s = [sources_of(fast_peer(j)) for j in range(1, fast)]
    mine = sources_of(me)
    held_f = [a * fast + lax.rem(b + fast - j, fast) for j in range(1, fast)]
    held_s = [lax.rem(a + slow - i, slow) * fast + b for i in range(1, slow)]
    from_f = []
    for i in range(1, slow):
        base = lax.rem(a + slow - i, slow) * fast
        from_f.append((mine >= base) & (mine < base + fast))
    from_s = []
    for j in range(1, fast):
        base = lax.rem(b + fast - j, fast)
        hit = mine == base
        for i in range(1, slow):
            hit = hit | (mine == base + i * fast)
        from_s.append(hit)
    for load in loads[1:]:
        load.wait()
    drag_halo(0).start()
    drag_halo(1).start()

    def pass_on(c):
        for j in range(1, fast):
            gather_f(j, c).wait_recv()
        for i in range(1, slow):
            for f in range(PAIR):
                for kk in range(CHUNK):
                    k = c * CHUNK + kk
                    value = ens[0, f, k]
                    for j in range(1, fast):
                        value = jnp.where(wanted_f[i - 1] == held_f[j - 1], ag_f[j - 1, f, k], value)
                    tx_f[i - 1, f, k] = value
            onward_f(i, c).start()
        for i in range(1, slow):
            gather_s(i, c).wait_recv()
        for j in range(1, fast):
            for f in range(PAIR):
                for kk in range(CHUNK):
                    k = c * CHUNK + kk
                    value = ens[0, PAIR + f, k]
                    for i in range(1, slow):
                        value = jnp.where(wanted_s[j - 1] == held_s[i - 1], ag_s[i - 1, f, k], value)
                    tx_s[j - 1, f, k] = value
            onward_s(j, c).start()

        @pl.when(c + AHEAD < chunks)
        def _():
            start_gather(c + AHEAD)

    blank = jnp.zeros((rows, cols), jnp.float32)

    def place_of(tile, f, kk):
        return 2 * ((tile * FIELDS + f) * CHUNK + kk)

    couple = lane >> 1

    def pack(q, place, packed):
        turned = pltpu.roll(q, (place + 1) % cols, 1)
        return jnp.where(couple == place // 2, turned, packed)

    def resample(c):
        for i in range(1, slow):
            onward_f(i, c).wait_recv()
        for j in range(1, fast):
            onward_s(j, c).wait_recv()
        for kk in range(CHUNK):
            k = c * CHUNK + kk
            for f in range(FIELDS):
                q = ens[0, f, k]
                if f < PAIR:
                    for j in range(1, fast):
                        q = jnp.where(mine == held_f[j - 1], ag_f[j - 1, f, k], q)
                    for i in range(1, slow):
                        q = jnp.where(from_f[i - 1], rx_f[i - 1, f, k], q)
                else:
                    for i in range(1, slow):
                        q = jnp.where(mine == held_s[i - 1], ag_s[i - 1, f - PAIR, k], q)
                    for j in range(1, fast):
                        q = jnp.where(from_s[j - 1], rx_s[j - 1, f - PAIR, k], q)
                state_0[0, f, k] = q
        row_halo(0, c).start()
        row_halo(1, c).start()

    def first_columns(c):
        row_halo(0, c).wait_recv()
        row_halo(1, c).wait_recv()
        packed = blank
        for tile in range(2):
            for f in range(FIELDS):
                for kk in range(CHUNK):
                    packed = pack(state_0[tile, f, c * CHUNK + kk], place_of(tile, f, kk), packed)
        hy_out[0, c] = packed
        start_columns(0, c)

    positions = (gy * cols + lane).astype(jnp.float32)
    coriolis = CORIO_BASE + CORIO_SLOPE * (positions + 0.5) / (n_gy * cols)
    half = 0.5 * ADVECT
    temp, salt = 0.5 * PRESS_SCALE * BUOY_TEMP, 0.5 * PRESS_SCALE * BUOY_SALT

    def advance(step, c):
        final = step == STEPS - 1
        now_ref, later_ref = states[step], None if final else states[step + 1]
        tiles = (0,) if final else (0, 1)
        wait_columns(step, c)
        columns = jnp.where(lane % 2 == 0, hy_in[step, 0, c], hy_in[step, 1, c])
        packed = blank
        press_x = [sums[step, t, 0] for t in tiles]
        press_y = [sums[step, t, 1] for t in tiles]
        flux = [[sums[step, t, 2 + f] for f in range(FIELDS)] for t in tiles]
        for kk in range(CHUNK):
            k = c * CHUNK + kk
            below = jnp.minimum(k + 1, levels - 1)
            mixing = eddy[jnp.minimum(k, levels - 2)]
            now = [[now_ref[t, f, k] for f in range(FIELDS)] for t in (0, 1)]
            result = [[None] * FIELDS for t in tiles]
            coef = []
            for t in tiles:
                u, v = now[t][0], now[t][1]
                coef.append((DIFFUSE + half * u, DIFFUSE - half * u, DIFFUSE + half * v, DIFFUSE - half * v))
            diff_x, diff_y = [[] for t in tiles], [[] for t in tiles]
            for f in range(FIELDS):
                up = [pltpu.roll(now[t][f], 1, 0) for t in (0, 1)]
                down = [pltpu.roll(now[t][f], rows - 1, 0) for t in (0, 1)]
                for t in tiles:
                    q = now[t][f]
                    x_m = jnp.where(row == 0, up[1 - t], up[t])
                    x_p = jnp.where(row == rows - 1, down[1 - t], down[t])
                    edge = pltpu.roll(columns, cols - 1 - place_of(t, f, kk), 1)
                    y_m = pltpu.roll(jnp.where(lane == cols - 1, edge, q), 1, 1)
                    y_p = pltpu.roll(jnp.where(lane == 0, edge, q), cols - 1, 1)
                    flow = mixing * (now_ref[t, f, below] - q)
                    total = (1.0 - 4.0 * DIFFUSE) * q + (flow - flux[t][f])
                    c_xm, c_xp, c_ym, c_yp = coef[t]
                    total = total + (c_xp * x_p + c_xm * x_m) + (c_yp * y_p + c_ym * y_m)
                    result[t][f] = total
                    flux[t][f] = flow
                    if f >= PAIR:
                        diff_x[t].append(x_p - x_m)
                        diff_y[t].append(y_p - y_m)
            for t in tiles:
                press_x[t] = press_x[t] + (temp * diff_x[t][0] - salt * diff_x[t][1])
                press_y[t] = press_y[t] + (temp * diff_y[t][0] - salt * diff_y[t][1])
                result[t][0] = result[t][0] + (coriolis * now[t][1] - press_x[t])
                result[t][1] = result[t][1] - (coriolis * now[t][0] + press_y[t])
                if kk == 0:
                    top = jnp.where(c == 0, WIND_SCALE, 0.0)
                    result[t][0] = result[t][0] + top * drag[t, 0]
                    result[t][1] = result[t][1] + top * drag[t, 1]
                for f in range(FIELDS):
                    if final:
                        out[0, f, k] = result[t][f]
                    else:
                        later_ref[t, f, k] = result[t][f]
                        packed = pack(result[t][f], place_of(t, f, kk), packed)
        for t in tiles:
            sums[step, t, 0] = press_x[t]
            sums[step, t, 1] = press_y[t]
            for f in range(FIELDS):
                sums[step, t, 2 + f] = flux[t][f]
        if final:
            write_out(c).start()
        else:
            hy_out[step + 1, c] = packed
            start_columns(step + 1, c)

    drag_halo(0).wait_recv()
    drag_halo(1).wait_recv()

    def tick(t, _):
        def at(c, body):
            @pl.when((c >= 0) & (c < chunks))
            def _():
                body(c)

        at(t, pass_on)
        at(t - 1, resample)
        at(t - 2, first_columns)

        for step in range(STEPS):
            at(t - 3 - step, functools.partial(advance, step))
        return 0

    lax.fori_loop(0, chunks + STEPS + 2, tick, 0)

    def drain(c, _):
        for j in range(1, fast):
            gather_f(j, c).wait_send()
            onward_s(j, c).wait_send()
        for i in range(1, slow):
            gather_s(i, c).wait_send()
            onward_f(i, c).wait_send()
        row_halo(0, c).wait_send()
        row_halo(1, c).wait_send()
        write_out(c).wait()
        for step in range(STEPS):
            @pl.when(has_right)
            def _():
                col_halo(step, 0, c).wait_send()

            @pl.when(has_left)
            def _():
                col_halo(step, 1, c).wait_send()

        return 0

    lax.fori_loop(0, chunks, drain, 0)
    drag_halo(0).wait_send()
    drag_halo(1).wait_send()


def per_device(slow, fast, n_gx, n_gy, ensemble, ancestors, particle_air_drag, eddy_diffusivity):
    levels, rows, cols = ensemble.shape[2:]
    chunks = levels // CHUNK
    block = (PAIR, levels, rows, cols)
    hbm = pl.BlockSpec(memory_space=pltpu.HBM)
    dma = pltpu.SemaphoreType.DMA
    f32 = jnp.float32
    return pl.pallas_call(
        functools.partial(kernel, slow, fast, n_gx, n_gy),
        out_shape=jax.ShapeDtypeStruct(ensemble.shape, f32),
        in_specs=[hbm] * 4,
        out_specs=hbm,
        scratch_shapes=[
            pltpu.VMEM(ensemble.shape, f32),
            pltpu.SMEM(ancestors.shape, jnp.int32),
            pltpu.VMEM((2,) + particle_air_drag.shape[1:], f32),
            pltpu.SMEM(eddy_diffusivity.shape, f32),
            pltpu.VMEM(ensemble.shape, f32),
            *[pltpu.VMEM((2, FIELDS, levels, rows, cols), f32)] * STEPS,
            pltpu.VMEM((STEPS, 2, 2 + FIELDS, rows, cols), f32),
            pltpu.VMEM((fast - 1,) + block, f32),
            pltpu.VMEM((slow - 1,) + block, f32),
            pltpu.VMEM((slow - 1,) + block, f32),
            pltpu.VMEM((fast - 1,) + block, f32),
            pltpu.VMEM((slow - 1,) + block, f32),
            pltpu.VMEM((fast - 1,) + block, f32),
            pltpu.VMEM((STEPS, chunks, rows, cols), f32),
            pltpu.VMEM((STEPS, 2, chunks, rows, cols), f32),
            dma((4,)),
            dma((chunks,)),
            dma((fast - 1, chunks)),
            dma((fast - 1, chunks)),
            dma((slow - 1, chunks)),
            dma((slow - 1, chunks)),
            dma((slow - 1, chunks)),
            dma((slow - 1, chunks)),
            dma((fast - 1, chunks)),
            dma((fast - 1, chunks)),
            dma((2, chunks)),
            dma((2, chunks)),
            dma((STEPS, 2, chunks)),
            dma((STEPS, 2, chunks)),
            dma((2,)),
            dma((2,)),
        ],
        compiler_params=pltpu.CompilerParams(
            collective_id=0, has_side_effects=True, vmem_limit_bytes=64 * 1024 * 1024
        ),
        cost_estimate=pl.CostEstimate(
            flops=STEPS * 60 * math.prod(ensemble.shape),
            bytes_accessed=8 * math.prod(ensemble.shape),
            transcendentals=0,
        ),
    )(ensemble, ancestors, particle_air_drag, eddy_diffusivity)


def solution(mesh):
    members = mesh.shape["dom"]
    fast = max(n for n in range(1, math.isqrt(members) + 1) if members % n == 0)
    placed = (
        P("dom", None, None, "gx", "gy"),
        P(None, "gx", "gy"),
        P("dom", None, "gx", "gy"),
        P(),
    )
    return jax.shard_map(
        functools.partial(
            per_device, members // fast, fast, mesh.shape["gx"], mesh.shape["gy"]
        ),
        mesh=mesh,
        in_specs=placed,
        out_specs=P("dom", None, None, "gx", "gy"),
        check_vma=False,
    )
```

```python
import functools
import math

import jax
import jax.numpy as jnp
from jax import lax
from jax.experimental import pallas as pl
from jax.experimental.pallas import tpu as pltpu
from jax.sharding import PartitionSpec as P

STEPS = 4
TILE = 8
CHUNK = 4
AHEAD = 3

ADVECT = 0.2
DIFFUSE = 0.15
BUOY_TEMP = 0.2
BUOY_SALT = 0.1
PRESS_SCALE = 0.25
WIND_SCALE = 0.2
CORIO_BASE = 0.1
CORIO_SLOPE = 0.1

MESH = pl.DeviceIdType.MESH
FIELDS = 4
PAIR = 2


def remote(src, dst, send, recv, where):
    return pltpu.make_async_remote_copy(
        src_ref=src,
        dst_ref=dst,
        send_sem=send,
        recv_sem=recv,
        device_id=where,
        device_id_type=MESH,
    )


def kernel(
    slow, fast, n_gx, n_gy, ens_hbm, anc_hbm, drag_hbm, eddy_hbm, out_hbm,
    ens, anc, drag, eddy, out, state_0, state_1, state_2, state_3, sums, ag_f, ag_s, tx_f, tx_s, rx_f, rx_s, hy_out, hy_in,
    local_sem, out_sem, agf_send, agf_recv, ags_send, ags_recv, txf_send, txf_recv, txs_send, txs_recv,
    hx_send, hx_recv, hy_send, hy_recv, drag_send, drag_recv,
):
    levels, rows, cols = ens.shape[2:]
    chunks = levels // CHUNK
    states = (state_0, state_1, state_2, state_3)
    me = lax.axis_index("dom")
    a, b = me // fast, me % fast
    gx, gy = lax.axis_index("gx"), lax.axis_index("gy")
    gx_next, gx_prev = lax.rem(gx + 1, n_gx), lax.rem(gx + n_gx - 1, n_gx)
    has_left, has_right = gy > 0, gy < n_gy - 1

    loads = [
        pltpu.make_async_copy(there, here, local_sem.at[number])
        for number, (there, here) in enumerate(
            ((anc_hbm, anc), (ens_hbm, ens), (eddy_hbm, eddy), (drag_hbm.at[0], drag.at[0]))
        )
    ]
    for load in loads:
        load.start()

    fast_peers = [a * fast + lax.rem(b + j, fast) for j in range(1, fast)]
    slow_peers = [lax.rem(a + i, slow) * fast + b for i in range(1, slow)]

    def fast_peer(j):
        return fast_peers[j - 1]

    def slow_peer(i):
        return slow_peers[i - 1]

    def at_dom(member):
        return (member, gx, gy)

    at_prev, at_next = (me, gx_prev, gy), (me, gx_next, gy)
    at_left, at_right = (me, gx, gy - 1), (me, gx, gy + 1)

    barrier = pltpu.get_barrier_semaphore()
    for j in range(1, fast):
        pl.semaphore_signal(barrier, inc=1, device_id=at_dom(fast_peer(j)), device_id_type=MESH)
    for i in range(1, slow):
        pl.semaphore_signal(barrier, inc=1, device_id=at_dom(slow_peer(i)), device_id_type=MESH)
    for there in (at_next, at_prev):
        pl.semaphore_signal(barrier, inc=1, device_id=there, device_id_type=MESH)

    @pl.when(has_left)
    def _():
        pl.semaphore_signal(barrier, inc=1, device_id=at_left, device_id_type=MESH)

    @pl.when(has_right)
    def _():
        pl.semaphore_signal(barrier, inc=1, device_id=at_right, device_id_type=MESH)

    around = has_left.astype(jnp.int32) + has_right.astype(jnp.int32)
    pl.semaphore_wait(barrier, fast - 1 + slow - 1 + 2 + around)

    def part(c):
        return pl.ds(c * CHUNK, CHUNK)

    def gather_f(j, c):
        return remote(ens.at[0, 0:PAIR, part(c)], ag_f.at[j - 1, :, part(c)],
                      agf_send.at[j - 1, c], agf_recv.at[j - 1, c], at_dom(fast_peer(j)))

    def gather_s(i, c):
        return remote(ens.at[0, PAIR:FIELDS, part(c)], ag_s.at[i - 1, :, part(c)],
                      ags_send.at[i - 1, c], ags_recv.at[i - 1, c], at_dom(slow_peer(i)))

    def onward_f(i, c):
        return remote(tx_f.at[i - 1, :, part(c)], rx_f.at[i - 1, :, part(c)],
                      txf_send.at[i - 1, c], txf_recv.at[i - 1, c], at_dom(slow_peer(i)))

    def onward_s(j, c):
        return remote(tx_s.at[j - 1, :, part(c)], rx_s.at[j - 1, :, part(c)],
                      txs_send.at[j - 1, c], txs_recv.at[j - 1, c], at_dom(fast_peer(j)))

    def row_halo(side, c):
        there = at_prev if side == 0 else at_next
        edge = slice(0, STEPS) if side == 0 else slice(rows - STEPS, rows)
        return remote(state_0.at[0, :, part(c), edge], state_0.at[1, :, part(c), edge],
                      hx_send.at[side, c], hx_recv.at[side, c], there)

    def drag_halo(side):
        there = at_prev if side == 0 else at_next
        edge = slice(0, STEPS) if side == 0 else slice(rows - STEPS, rows)
        return remote(drag.at[0, :, edge], drag.at[1, :, edge],
                      drag_send.at[side], drag_recv.at[side], there)

    def col_halo(step, side, c):
        there = at_right if side == 0 else at_left
        return remote(hy_out.at[step, c], hy_in.at[step, side, c],
                      hy_send.at[step, side, c], hy_recv.at[step, side, c], there)

    def write_out(c):
        return pltpu.make_async_copy(out.at[:, :, part(c)], out_hbm.at[:, :, part(c)], out_sem.at[c])

    def start_columns(step, c):
        @pl.when(has_right)
        def _():
            col_halo(step, 0, c).start()

        @pl.when(has_left)
        def _():
            col_halo(step, 1, c).start()

    def wait_columns(step, c):
        @pl.when(has_left)
        def _():
            col_halo(step, 0, c).wait_recv()

        @pl.when(has_right)
        def _():
            col_halo(step, 1, c).wait_recv()

    def start_gather(c):
        for j in range(1, fast):
            gather_f(j, c).start()
        for i in range(1, slow):
            gather_s(i, c).start()

    loads[1].wait()
    for c in range(min(AHEAD, chunks)):
        start_gather(c)

    @pl.when(jnp.logical_not(has_left))
    def _():
        hy_in[:, 0] = jnp.zeros((STEPS, chunks, rows, cols), jnp.float32)

    @pl.when(jnp.logical_not(has_right))
    def _():
        hy_in[:, 1] = jnp.zeros((STEPS, chunks, rows, cols), jnp.float32)

    sums[...] = jnp.zeros(sums.shape, jnp.float32)
    row = lax.broadcasted_iota(jnp.int32, (rows, cols), 0)
    lane = lax.broadcasted_iota(jnp.int32, (rows, cols), 1)
    loads[0].wait()

    def sources_of(member):
        total = jnp.zeros((rows, cols), jnp.int32)
        for tx in range(rows // TILE):
            for ty in range(cols // TILE):
                here = (lane >= ty * TILE) & (lane < (ty + 1) * TILE)
                if rows > TILE:
                    here = here & (row >= tx * TILE) & (row < (tx + 1) * TILE)
                total = jnp.where(here, anc[member, tx, ty], total)
        return total

    wanted_f = [sources_of(slow_peer(i)) for i in range(1, slow)]
    wanted_s = [sources_of(fast_peer(j)) for j in range(1, fast)]
    mine = sources_of(me)
    held_f = [a * fast + lax.rem(b + fast - j, fast) for j in range(1, fast)]
    held_s = [lax.rem(a + slow - i, slow) * fast + b for i in range(1, slow)]
    from_f = []
    for i in range(1, slow):
        base = lax.rem(a + slow - i, slow) * fast
        from_f.append((mine >= base) & (mine < base + fast))
    from_s = []
    for j in range(1, fast):
        base = lax.rem(b + fast - j, fast)
        hit = mine == base
        for i in range(1, slow):
            hit = hit | (mine == base + i * fast)
        from_s.append(hit)
    for load in loads[2:]:
        load.wait()
    drag_halo(0).start()
    drag_halo(1).start()

    def pass_on(c):
        for j in range(1, fast):
            gather_f(j, c).wait_recv()
        for i in range(1, slow):
            for f in range(PAIR):
                for kk in range(CHUNK):
                    k = c * CHUNK + kk
                    value = ens[0, f, k]
                    for j in range(1, fast):
                        value = jnp.where(wanted_f[i - 1] == held_f[j - 1], ag_f[j - 1, f, k], value)
                    tx_f[i - 1, f, k] = value
            onward_f(i, c).start()
        for i in range(1, slow):
            gather_s(i, c).wait_recv()
        for j in range(1, fast):
            for f in range(PAIR):
                for kk in range(CHUNK):
                    k = c * CHUNK + kk
                    value = ens[0, PAIR + f, k]
                    for i in range(1, slow):
                        value = jnp.where(wanted_s[j - 1] == held_s[i - 1], ag_s[i - 1, f, k], value)
                    tx_s[j - 1, f, k] = value
            onward_s(j, c).start()

        @pl.when(c + AHEAD < chunks)
        def _():
            start_gather(c + AHEAD)

    blank = jnp.zeros((rows, cols), jnp.float32)

    def place_of(tile, f, kk):
        return 2 * ((tile * FIELDS + f) * CHUNK + kk)

    couple = lane >> 1

    def pack(q, place, packed):
        turned = pltpu.roll(q, (place + 1) % cols, 1)
        return jnp.where(couple == place // 2, turned, packed)

    def resample(c):
        for i in range(1, slow):
            onward_f(i, c).wait_recv()
        for j in range(1, fast):
            onward_s(j, c).wait_recv()
        for kk in range(CHUNK):
            k = c * CHUNK + kk
            for f in range(FIELDS):
                q = ens[0, f, k]
                if f < PAIR:
                    for j in range(1, fast):
                        q = jnp.where(mine == held_f[j - 1], ag_f[j - 1, f, k], q)
                    for i in range(1, slow):
                        q = jnp.where(from_f[i - 1], rx_f[i - 1, f, k], q)
                else:
                    for i in range(1, slow):
                        q = jnp.where(mine == held_s[i - 1], ag_s[i - 1, f - PAIR, k], q)
                    for j in range(1, fast):
                        q = jnp.where(from_s[j - 1], rx_s[j - 1, f - PAIR, k], q)
                state_0[0, f, k] = q
        row_halo(0, c).start()
        row_halo(1, c).start()

    def first_columns(c):
        row_halo(0, c).wait_recv()
        row_halo(1, c).wait_recv()
        packed = blank
        for tile in range(2):
            for f in range(FIELDS):
                for kk in range(CHUNK):
                    packed = pack(state_0[tile, f, c * CHUNK + kk], place_of(tile, f, kk), packed)
        hy_out[0, c] = packed
        start_columns(0, c)

    positions = (gy * cols + lane).astype(jnp.float32)
    coriolis = CORIO_BASE + CORIO_SLOPE * (positions + 0.5) / (n_gy * cols)
    half = 0.5 * ADVECT
    temp, salt = 0.5 * PRESS_SCALE * BUOY_TEMP, 0.5 * PRESS_SCALE * BUOY_SALT

    def advance(step, c):
        final = step == STEPS - 1
        now_ref, later_ref = states[step], None if final else states[step + 1]
        tiles = (0,) if final else (0, 1)
        wait_columns(step, c)
        columns = jnp.where(lane % 2 == 0, hy_in[step, 0, c], hy_in[step, 1, c])
        packed = blank
        press_x = [sums[step, t, 0] for t in tiles]
        press_y = [sums[step, t, 1] for t in tiles]
        flux = [[sums[step, t, 2 + f] for f in range(FIELDS)] for t in tiles]
        for kk in range(CHUNK):
            k = c * CHUNK + kk
            below = jnp.minimum(k + 1, levels - 1)
            mixing = eddy[jnp.minimum(k, levels - 2)]
            now = [[now_ref[t, f, k] for f in range(FIELDS)] for t in (0, 1)]
            result = [[None] * FIELDS for t in tiles]
            coef = []
            for t in tiles:
                u, v = now[t][0], now[t][1]
                coef.append((DIFFUSE + half * u, DIFFUSE - half * u, DIFFUSE + half * v, DIFFUSE - half * v))
            diff_x, diff_y = [[] for t in tiles], [[] for t in tiles]
            for f in range(FIELDS):
                up = [pltpu.roll(now[t][f], 1, 0) for t in (0, 1)]
                down = [pltpu.roll(now[t][f], rows - 1, 0) for t in (0, 1)]
                for t in tiles:
                    q = now[t][f]
                    x_m = jnp.where(row == 0, up[1 - t], up[t])
                    x_p = jnp.where(row == rows - 1, down[1 - t], down[t])
                    edge = pltpu.roll(columns, cols - 1 - place_of(t, f, kk), 1)
                    y_m = pltpu.roll(jnp.where(lane == cols - 1, edge, q), 1, 1)
                    y_p = pltpu.roll(jnp.where(lane == 0, edge, q), cols - 1, 1)
                    flow = mixing * (now_ref[t, f, below] - q)
                    total = (1.0 - 4.0 * DIFFUSE) * q + (flow - flux[t][f])
                    c_xm, c_xp, c_ym, c_yp = coef[t]
                    total = total + (c_xp * x_p + c_xm * x_m) + (c_yp * y_p + c_ym * y_m)
                    result[t][f] = total
                    flux[t][f] = flow
                    if f >= PAIR:
                        diff_x[t].append(x_p - x_m)
                        diff_y[t].append(y_p - y_m)
            for t in tiles:
                press_x[t] = press_x[t] + (temp * diff_x[t][0] - salt * diff_x[t][1])
                press_y[t] = press_y[t] + (temp * diff_y[t][0] - salt * diff_y[t][1])
                result[t][0] = result[t][0] + (coriolis * now[t][1] - press_x[t])
                result[t][1] = result[t][1] - (coriolis * now[t][0] + press_y[t])
                if kk == 0:
                    top = jnp.where(c == 0, WIND_SCALE, 0.0)
                    result[t][0] = result[t][0] + top * drag[t, 0]
                    result[t][1] = result[t][1] + top * drag[t, 1]
                for f in range(FIELDS):
                    if final:
                        out[0, f, k] = result[t][f]
                    else:
                        later_ref[t, f, k] = result[t][f]
                        packed = pack(result[t][f], place_of(t, f, kk), packed)
        for t in tiles:
            sums[step, t, 0] = press_x[t]
            sums[step, t, 1] = press_y[t]
            for f in range(FIELDS):
                sums[step, t, 2 + f] = flux[t][f]
        if final:
            write_out(c).start()
        else:
            hy_out[step + 1, c] = packed
            start_columns(step + 1, c)

    drag_halo(0).wait_recv()
    drag_halo(1).wait_recv()

    def tick(t, _):
        def at(c, body):
            @pl.when((c >= 0) & (c < chunks))
            def _():
                body(c)

        at(t, pass_on)
        at(t - 1, resample)
        at(t - 2, first_columns)

        for step in range(STEPS):
            at(t - 3 - step, functools.partial(advance, step))
        return 0

    lax.fori_loop(0, chunks + STEPS + 2, tick, 0)

    def drain(c, _):
        for j in range(1, fast):
            gather_f(j, c).wait_send()
            onward_s(j, c).wait_send()
        for i in range(1, slow):
            gather_s(i, c).wait_send()
            onward_f(i, c).wait_send()
        row_halo(0, c).wait_send()
        row_halo(1, c).wait_send()
        write_out(c).wait()
        for step in range(STEPS):
            @pl.when(has_right)
            def _():
                col_halo(step, 0, c).wait_send()

            @pl.when(has_left)
            def _():
                col_halo(step, 1, c).wait_send()

        return 0

    lax.fori_loop(0, chunks, drain, 0)
    drag_halo(0).wait_send()
    drag_halo(1).wait_send()


def per_device(slow, fast, n_gx, n_gy, ensemble, ancestors, particle_air_drag, eddy_diffusivity):
    levels, rows, cols = ensemble.shape[2:]
    chunks = levels // CHUNK
    block = (PAIR, levels, rows, cols)
    hbm = pl.BlockSpec(memory_space=pltpu.HBM)
    dma = pltpu.SemaphoreType.DMA
    f32 = jnp.float32
    return pl.pallas_call(
        functools.partial(kernel, slow, fast, n_gx, n_gy),
        out_shape=jax.ShapeDtypeStruct(ensemble.shape, f32),
        in_specs=[hbm] * 4,
        out_specs=hbm,
        scratch_shapes=[
            pltpu.VMEM(ensemble.shape, f32),
            pltpu.SMEM(ancestors.shape, jnp.int32),
            pltpu.VMEM((2,) + particle_air_drag.shape[1:], f32),
            pltpu.SMEM(eddy_diffusivity.shape, f32),
            pltpu.VMEM(ensemble.shape, f32),
            *[pltpu.VMEM((2, FIELDS, levels, rows, cols), f32)] * STEPS,
            pltpu.VMEM((STEPS, 2, 2 + FIELDS, rows, cols), f32),
            pltpu.VMEM((fast - 1,) + block, f32),
            pltpu.VMEM((slow - 1,) + block, f32),
            pltpu.VMEM((slow - 1,) + block, f32),
            pltpu.VMEM((fast - 1,) + block, f32),
            pltpu.VMEM((slow - 1,) + block, f32),
            pltpu.VMEM((fast - 1,) + block, f32),
            pltpu.VMEM((STEPS, chunks, rows, cols), f32),
            pltpu.VMEM((STEPS, 2, chunks, rows, cols), f32),
            dma((4,)),
            dma((chunks,)),
            dma((fast - 1, chunks)),
            dma((fast - 1, chunks)),
            dma((slow - 1, chunks)),
            dma((slow - 1, chunks)),
            dma((slow - 1, chunks)),
            dma((slow - 1, chunks)),
            dma((fast - 1, chunks)),
            dma((fast - 1, chunks)),
            dma((2, chunks)),
            dma((2, chunks)),
            dma((STEPS, 2, chunks)),
            dma((STEPS, 2, chunks)),
            dma((2,)),
            dma((2,)),
        ],
        compiler_params=pltpu.CompilerParams(
            collective_id=0, has_side_effects=True, vmem_limit_bytes=64 * 1024 * 1024
        ),
        cost_estimate=pl.CostEstimate(
            flops=STEPS * 60 * math.prod(ensemble.shape),
            bytes_accessed=8 * math.prod(ensemble.shape),
            transcendentals=0,
        ),
    )(ensemble, ancestors, particle_air_drag, eddy_diffusivity)


def solution(mesh):
    members = mesh.shape["dom"]
    fast = max(n for n in range(1, math.isqrt(members) + 1) if members % n == 0)
    placed = (
        P("dom", None, None, "gx", "gy"),
        P(None, "gx", "gy"),
        P("dom", None, "gx", "gy"),
        P(),
    )
    return jax.shard_map(
        functools.partial(
            per_device, members // fast, fast, mesh.shape["gx"], mesh.shape["gy"]
        ),
        mesh=mesh,
        in_specs=placed,
        out_specs=P("dom", None, None, "gx", "gy"),
        check_vma=False,
    )
```

```python
import functools
import math

import jax
import jax.numpy as jnp
from jax import lax
from jax.experimental import pallas as pl
from jax.experimental.pallas import tpu as pltpu
from jax.sharding import PartitionSpec as P

STEPS = 4
TILE = 8
CHUNK = 8
AHEAD = 2

ADVECT = 0.2
DIFFUSE = 0.15
BUOY_TEMP = 0.2
BUOY_SALT = 0.1
PRESS_SCALE = 0.25
WIND_SCALE = 0.2
CORIO_BASE = 0.1
CORIO_SLOPE = 0.1

MESH = pl.DeviceIdType.MESH
FIELDS = 4
PAIR = 2


def remote(src, dst, send, recv, where):
    return pltpu.make_async_remote_copy(
        src_ref=src,
        dst_ref=dst,
        send_sem=send,
        recv_sem=recv,
        device_id=where,
        device_id_type=MESH,
    )


def kernel(
    slow, fast, n_gx, n_gy, ens_hbm, anc_hbm, drag_hbm, eddy_hbm, out_hbm,
    ens, anc, drag, eddy, out, state_0, state_1, state_2, state_3, sums, ag_f, ag_s, tx_f, tx_s, rx_f, rx_s, hy_out, hy_in,
    local_sem, out_sem, agf_send, agf_recv, ags_send, ags_recv, txf_send, txf_recv, txs_send, txs_recv,
    hx_send, hx_recv, hy_send, hy_recv, drag_send, drag_recv,
):
    levels, rows, cols = ens.shape[2:]
    chunks = levels // CHUNK
    states = (state_0, state_1, state_2, state_3)
    me = lax.axis_index("dom")
    a, b = me // fast, me % fast
    gx, gy = lax.axis_index("gx"), lax.axis_index("gy")
    gx_next, gx_prev = lax.rem(gx + 1, n_gx), lax.rem(gx + n_gx - 1, n_gx)
    has_left, has_right = gy > 0, gy < n_gy - 1

    loads = [
        pltpu.make_async_copy(there, here, local_sem.at[number])
        for number, (there, here) in enumerate(
            ((anc_hbm, anc), (ens_hbm, ens), (eddy_hbm, eddy), (drag_hbm.at[0], drag.at[0]))
        )
    ]
    for load in loads:
        load.start()

    fast_peers = [a * fast + lax.rem(b + j, fast) for j in range(1, fast)]
    slow_peers = [lax.rem(a + i, slow) * fast + b for i in range(1, slow)]

    def fast_peer(j):
        return fast_peers[j - 1]

    def slow_peer(i):
        return slow_peers[i - 1]

    def at_dom(member):
        return (member, gx, gy)

    at_prev, at_next = (me, gx_prev, gy), (me, gx_next, gy)
    at_left, at_right = (me, gx, gy - 1), (me, gx, gy + 1)

    barrier = pltpu.get_barrier_semaphore()
    for j in range(1, fast):
        pl.semaphore_signal(barrier, inc=1, device_id=at_dom(fast_peer(j)), device_id_type=MESH)
    for i in range(1, slow):
        pl.semaphore_signal(barrier, inc=1, device_id=at_dom(slow_peer(i)), device_id_type=MESH)
    for there in (at_next, at_prev):
        pl.semaphore_signal(barrier, inc=1, device_id=there, device_id_type=MESH)

    @pl.when(has_left)
    def _():
        pl.semaphore_signal(barrier, inc=1, device_id=at_left, device_id_type=MESH)

    @pl.when(has_right)
    def _():
        pl.semaphore_signal(barrier, inc=1, device_id=at_right, device_id_type=MESH)

    around = has_left.astype(jnp.int32) + has_right.astype(jnp.int32)
    pl.semaphore_wait(barrier, fast - 1 + slow - 1 + 2 + around)

    def part(c):
        return pl.ds(c * CHUNK, CHUNK)

    def gather_f(j, c):
        return remote(ens.at[0, 0:PAIR, part(c)], ag_f.at[j - 1, :, part(c)],
                      agf_send.at[j - 1, c], agf_recv.at[j - 1, c], at_dom(fast_peer(j)))

    def gather_s(i, c):
        return remote(ens.at[0, PAIR:FIELDS, part(c)], ag_s.at[i - 1, :, part(c)],
                      ags_send.at[i - 1, c], ags_recv.at[i - 1, c], at_dom(slow_peer(i)))

    def onward_f(i, c):
        return remote(tx_f.at[i - 1, :, part(c)], rx_f.at[i - 1, :, part(c)],
                      txf_send.at[i - 1, c], txf_recv.at[i - 1, c], at_dom(slow_peer(i)))

    def onward_s(j, c):
        return remote(tx_s.at[j - 1, :, part(c)], rx_s.at[j - 1, :, part(c)],
                      txs_send.at[j - 1, c], txs_recv.at[j - 1, c], at_dom(fast_peer(j)))

    def row_halo(side, c):
        there = at_prev if side == 0 else at_next
        edge = slice(0, STEPS) if side == 0 else slice(rows - STEPS, rows)
        return remote(state_0.at[0, :, part(c), edge], state_0.at[1, :, part(c), edge],
                      hx_send.at[side, c], hx_recv.at[side, c], there)

    def drag_halo(side):
        there = at_prev if side == 0 else at_next
        edge = slice(0, STEPS) if side == 0 else slice(rows - STEPS, rows)
        return remote(drag.at[0, :, edge], drag.at[1, :, edge],
                      drag_send.at[side], drag_recv.at[side], there)

    def col_halo(step, side, c):
        there = at_right if side == 0 else at_left
        return remote(hy_out.at[step, c], hy_in.at[step, side, c],
                      hy_send.at[step, side, c], hy_recv.at[step, side, c], there)

    def write_out(c):
        return pltpu.make_async_copy(out.at[:, :, part(c)], out_hbm.at[:, :, part(c)], out_sem.at[c])

    def start_columns(step, c):
        @pl.when(has_right)
        def _():
            col_halo(step, 0, c).start()

        @pl.when(has_left)
        def _():
            col_halo(step, 1, c).start()

    def wait_columns(step, c):
        @pl.when(has_left)
        def _():
            col_halo(step, 0, c).wait_recv()

        @pl.when(has_right)
        def _():
            col_halo(step, 1, c).wait_recv()

    def start_gather(c):
        for j in range(1, fast):
            gather_f(j, c).start()
        for i in range(1, slow):
            gather_s(i, c).start()

    loads[1].wait()
    for c in range(min(AHEAD, chunks)):
        start_gather(c)

    @pl.when(jnp.logical_not(has_left))
    def _():
        hy_in[:, 0] = jnp.zeros((STEPS, chunks, rows, cols), jnp.float32)

    @pl.when(jnp.logical_not(has_right))
    def _():
        hy_in[:, 1] = jnp.zeros((STEPS, chunks, rows, cols), jnp.float32)

    sums[...] = jnp.zeros(sums.shape, jnp.float32)
    row = lax.broadcasted_iota(jnp.int32, (rows, cols), 0)
    lane = lax.broadcasted_iota(jnp.int32, (rows, cols), 1)
    loads[0].wait()

    def sources_of(member):
        total = jnp.zeros((rows, cols), jnp.int32)
        for tx in range(rows // TILE):
            for ty in range(cols // TILE):
                here = (lane >= ty * TILE) & (lane < (ty + 1) * TILE)
                if rows > TILE:
                    here = here & (row >= tx * TILE) & (row < (tx + 1) * TILE)
                total = jnp.where(here, anc[member, tx, ty], total)
        return total

    wanted_f = [sources_of(slow_peer(i)) for i in range(1, slow)]
    wanted_s = [sources_of(fast_peer(j)) for j in range(1, fast)]
    mine = sources_of(me)
    held_f = [a * fast + lax.rem(b + fast - j, fast) for j in range(1, fast)]
    held_s = [lax.rem(a + slow - i, slow) * fast + b for i in range(1, slow)]
    from_f = []
    for i in range(1, slow):
        base = lax.rem(a + slow - i, slow) * fast
        from_f.append((mine >= base) & (mine < base + fast))
    from_s = []
    for j in range(1, fast):
        base = lax.rem(b + fast - j, fast)
        hit = mine == base
        for i in range(1, slow):
            hit = hit | (mine == base + i * fast)
        from_s.append(hit)
    for load in loads[2:]:
        load.wait()
    drag_halo(0).start()
    drag_halo(1).start()

    def pass_on(c):
        for j in range(1, fast):
            gather_f(j, c).wait_recv()
        for i in range(1, slow):
            for f in range(PAIR):
                for kk in range(CHUNK):
                    k = c * CHUNK + kk
                    value = ens[0, f, k]
                    for j in range(1, fast):
                        value = jnp.where(wanted_f[i - 1] == held_f[j - 1], ag_f[j - 1, f, k], value)
                    tx_f[i - 1, f, k] = value
            onward_f(i, c).start()
        for i in range(1, slow):
            gather_s(i, c).wait_recv()
        for j in range(1, fast):
            for f in range(PAIR):
                for kk in range(CHUNK):
                    k = c * CHUNK + kk
                    value = ens[0, PAIR + f, k]
                    for i in range(1, slow):
                        value = jnp.where(wanted_s[j - 1] == held_s[i - 1], ag_s[i - 1, f, k], value)
                    tx_s[j - 1, f, k] = value
            onward_s(j, c).start()

        @pl.when(c + AHEAD < chunks)
        def _():
            start_gather(c + AHEAD)

    blank = jnp.zeros((rows, cols), jnp.float32)

    def place_of(tile, f, kk):
        return 2 * ((tile * FIELDS + f) * CHUNK + kk)

    couple = lane >> 1

    def pack(q, place, packed):
        turned = pltpu.roll(q, (place + 1) % cols, 1)
        return jnp.where(couple == place // 2, turned, packed)

    def resample(c):
        for i in range(1, slow):
            onward_f(i, c).wait_recv()
        for j in range(1, fast):
            onward_s(j, c).wait_recv()
        for kk in range(CHUNK):
            k = c * CHUNK + kk
            for f in range(FIELDS):
                q = ens[0, f, k]
                if f < PAIR:
                    for j in range(1, fast):
                        q = jnp.where(mine == held_f[j - 1], ag_f[j - 1, f, k], q)
                    for i in range(1, slow):
                        q = jnp.where(from_f[i - 1], rx_f[i - 1, f, k], q)
                else:
                    for i in range(1, slow):
                        q = jnp.where(mine == held_s[i - 1], ag_s[i - 1, f - PAIR, k], q)
                    for j in range(1, fast):
                        q = jnp.where(from_s[j - 1], rx_s[j - 1, f - PAIR, k], q)
                state_0[0, f, k] = q
        row_halo(0, c).start()
        row_halo(1, c).start()

    def first_columns(c):
        row_halo(0, c).wait_recv()
        row_halo(1, c).wait_recv()
        packed = blank
        for tile in range(2):
            for f in range(FIELDS):
                for kk in range(CHUNK):
                    packed = pack(state_0[tile, f, c * CHUNK + kk], place_of(tile, f, kk), packed)
        hy_out[0, c] = packed
        start_columns(0, c)

    positions = (gy * cols + lane).astype(jnp.float32)
    coriolis = CORIO_BASE + CORIO_SLOPE * (positions + 0.5) / (n_gy * cols)
    half = 0.5 * ADVECT
    temp, salt = 0.5 * PRESS_SCALE * BUOY_TEMP, 0.5 * PRESS_SCALE * BUOY_SALT

    def advance(step, c):
        final = step == STEPS - 1
        now_ref, later_ref = states[step], None if final else states[step + 1]
        tiles = (0,) if final else (0, 1)
        wait_columns(step, c)
        columns = jnp.where(lane % 2 == 0, hy_in[step, 0, c], hy_in[step, 1, c])
        packed = blank
        press_x = [sums[step, t, 0] for t in tiles]
        press_y = [sums[step, t, 1] for t in tiles]
        flux = [[sums[step, t, 2 + f] for f in range(FIELDS)] for t in tiles]
        for kk in range(CHUNK):
            k = c * CHUNK + kk
            below = jnp.minimum(k + 1, levels - 1)
            mixing = eddy[jnp.minimum(k, levels - 2)]
            now = [[now_ref[t, f, k] for f in range(FIELDS)] for t in (0, 1)]
            result = [[None] * FIELDS for t in tiles]
            coef = []
            for t in tiles:
                u, v = now[t][0], now[t][1]
                coef.append((DIFFUSE + half * u, DIFFUSE - half * u, DIFFUSE + half * v, DIFFUSE - half * v))
            diff_x, diff_y = [[] for t in tiles], [[] for t in tiles]
            for f in range(FIELDS):
                up = [pltpu.roll(now[t][f], 1, 0) for t in (0, 1)]
                down = [pltpu.roll(now[t][f], rows - 1, 0) for t in (0, 1)]
                for t in tiles:
                    q = now[t][f]
                    x_m = jnp.where(row == 0, up[1 - t], up[t])
                    x_p = jnp.where(row == rows - 1, down[1 - t], down[t])
                    edge = pltpu.roll(columns, cols - 1 - place_of(t, f, kk), 1)
                    y_m = pltpu.roll(jnp.where(lane == cols - 1, edge, q), 1, 1)
                    y_p = pltpu.roll(jnp.where(lane == 0, edge, q), cols - 1, 1)
                    flow = mixing * (now_ref[t, f, below] - q)
                    total = (1.0 - 4.0 * DIFFUSE) * q + (flow - flux[t][f])
                    c_xm, c_xp, c_ym, c_yp = coef[t]
                    total = total + (c_xp * x_p + c_xm * x_m) + (c_yp * y_p + c_ym * y_m)
                    result[t][f] = total
                    flux[t][f] = flow
                    if f >= PAIR:
                        diff_x[t].append(x_p - x_m)
                        diff_y[t].append(y_p - y_m)
            for t in tiles:
                press_x[t] = press_x[t] + (temp * diff_x[t][0] - salt * diff_x[t][1])
                press_y[t] = press_y[t] + (temp * diff_y[t][0] - salt * diff_y[t][1])
                result[t][0] = result[t][0] + (coriolis * now[t][1] - press_x[t])
                result[t][1] = result[t][1] - (coriolis * now[t][0] + press_y[t])
                if kk == 0:
                    top = jnp.where(c == 0, WIND_SCALE, 0.0)
                    result[t][0] = result[t][0] + top * drag[t, 0]
                    result[t][1] = result[t][1] + top * drag[t, 1]
                for f in range(FIELDS):
                    if final:
                        out[0, f, k] = result[t][f]
                    else:
                        later_ref[t, f, k] = result[t][f]
                        packed = pack(result[t][f], place_of(t, f, kk), packed)
        for t in tiles:
            sums[step, t, 0] = press_x[t]
            sums[step, t, 1] = press_y[t]
            for f in range(FIELDS):
                sums[step, t, 2 + f] = flux[t][f]
        if final:
            write_out(c).start()
        else:
            hy_out[step + 1, c] = packed
            start_columns(step + 1, c)

    drag_halo(0).wait_recv()
    drag_halo(1).wait_recv()

    def tick(t, _):
        def at(c, body):
            @pl.when((c >= 0) & (c < chunks))
            def _():
                body(c)

        at(t, pass_on)
        at(t - 1, resample)
        at(t - 2, first_columns)

        for step in range(STEPS):
            at(t - 3 - step, functools.partial(advance, step))
        return 0

    lax.fori_loop(0, chunks + STEPS + 2, tick, 0)

    def drain(c, _):
        for j in range(1, fast):
            gather_f(j, c).wait_send()
            onward_s(j, c).wait_send()
        for i in range(1, slow):
            gather_s(i, c).wait_send()
            onward_f(i, c).wait_send()
        row_halo(0, c).wait_send()
        row_halo(1, c).wait_send()
        write_out(c).wait()
        for step in range(STEPS):
            @pl.when(has_right)
            def _():
                col_halo(step, 0, c).wait_send()

            @pl.when(has_left)
            def _():
                col_halo(step, 1, c).wait_send()

        return 0

    lax.fori_loop(0, chunks, drain, 0)
    drag_halo(0).wait_send()
    drag_halo(1).wait_send()


def per_device(slow, fast, n_gx, n_gy, ensemble, ancestors, particle_air_drag, eddy_diffusivity):
    levels, rows, cols = ensemble.shape[2:]
    chunks = levels // CHUNK
    block = (PAIR, levels, rows, cols)
    hbm = pl.BlockSpec(memory_space=pltpu.HBM)
    dma = pltpu.SemaphoreType.DMA
    f32 = jnp.float32
    return pl.pallas_call(
        functools.partial(kernel, slow, fast, n_gx, n_gy),
        out_shape=jax.ShapeDtypeStruct(ensemble.shape, f32),
        in_specs=[hbm] * 4,
        out_specs=hbm,
        scratch_shapes=[
            pltpu.VMEM(ensemble.shape, f32),
            pltpu.SMEM(ancestors.shape, jnp.int32),
            pltpu.VMEM((2,) + particle_air_drag.shape[1:], f32),
            pltpu.SMEM(eddy_diffusivity.shape, f32),
            pltpu.VMEM(ensemble.shape, f32),
            *[pltpu.VMEM((2, FIELDS, levels, rows, cols), f32)] * STEPS,
            pltpu.VMEM((STEPS, 2, 2 + FIELDS, rows, cols), f32),
            pltpu.VMEM((fast - 1,) + block, f32),
            pltpu.VMEM((slow - 1,) + block, f32),
            pltpu.VMEM((slow - 1,) + block, f32),
            pltpu.VMEM((fast - 1,) + block, f32),
            pltpu.VMEM((slow - 1,) + block, f32),
            pltpu.VMEM((fast - 1,) + block, f32),
            pltpu.VMEM((STEPS, chunks, rows, cols), f32),
            pltpu.VMEM((STEPS, 2, chunks, rows, cols), f32),
            dma((4,)),
            dma((chunks,)),
            dma((fast - 1, chunks)),
            dma((fast - 1, chunks)),
            dma((slow - 1, chunks)),
            dma((slow - 1, chunks)),
            dma((slow - 1, chunks)),
            dma((slow - 1, chunks)),
            dma((fast - 1, chunks)),
            dma((fast - 1, chunks)),
            dma((2, chunks)),
            dma((2, chunks)),
            dma((STEPS, 2, chunks)),
            dma((STEPS, 2, chunks)),
            dma((2,)),
            dma((2,)),
        ],
        compiler_params=pltpu.CompilerParams(
            collective_id=0, has_side_effects=True, vmem_limit_bytes=32 * 1024 * 1024
        ),
        cost_estimate=pl.CostEstimate(
            flops=STEPS * 60 * math.prod(ensemble.shape),
            bytes_accessed=8 * math.prod(ensemble.shape),
            transcendentals=0,
        ),
    )(ensemble, ancestors, particle_air_drag, eddy_diffusivity)


def solution(mesh):
    members = mesh.shape["dom"]
    fast = max(n for n in range(1, math.isqrt(members) + 1) if members % n == 0)
    placed = (
        P("dom", None, None, "gx", "gy"),
        P(None, "gx", "gy"),
        P("dom", None, "gx", "gy"),
        P(),
    )
    return jax.shard_map(
        functools.partial(
            per_device, members // fast, fast, mesh.shape["gx"], mesh.shape["gy"]
        ),
        mesh=mesh,
        in_specs=placed,
        out_specs=P("dom", None, None, "gx", "gy"),
        check_vma=False,
    )
```

```python
import functools
import math

import jax
import jax.numpy as jnp
from jax import lax
from jax.experimental import pallas as pl
from jax.experimental.pallas import tpu as pltpu
from jax.sharding import PartitionSpec as P

STEPS = 4
TILE = 8
CHUNK = 8

ADVECT = 0.2
DIFFUSE = 0.15
BUOY_TEMP = 0.2
BUOY_SALT = 0.1
PRESS_SCALE = 0.25
WIND_SCALE = 0.2
CORIO_BASE = 0.1
CORIO_SLOPE = 0.1

MESH = pl.DeviceIdType.MESH
FIELDS = 4
PAIR = 2


def remote(src, dst, send, recv, where):
    return pltpu.make_async_remote_copy(
        src_ref=src,
        dst_ref=dst,
        send_sem=send,
        recv_sem=recv,
        device_id=where,
        device_id_type=MESH,
    )


def kernel(
    slow, fast, n_gx, n_gy, ens_hbm, anc_hbm, drag_hbm, eddy_hbm, out_hbm,
    ens, anc, drag, eddy, out, state, sums, ag_f, ag_s, tx_f, tx_s, rx_f, rx_s, hy_out, hy_in,
    local_sem, out_sem, agf_send, agf_recv, ags_send, ags_recv, txf_send, txf_recv, txs_send, txs_recv,
    hx_send, hx_recv, hy_send, hy_recv, drag_send, drag_recv,
):
    levels, rows, cols = ens.shape[2:]
    chunks = levels // CHUNK
    me = lax.axis_index("dom")
    a, b = me // fast, me % fast
    gx, gy = lax.axis_index("gx"), lax.axis_index("gy")
    gx_next, gx_prev = lax.rem(gx + 1, n_gx), lax.rem(gx + n_gx - 1, n_gx)
    has_left, has_right = gy > 0, gy < n_gy - 1

    loads = [
        pltpu.make_async_copy(there, here, local_sem.at[number])
        for number, (there, here) in enumerate(
            ((anc_hbm, anc), (ens_hbm, ens), (eddy_hbm, eddy), (drag_hbm.at[0], drag.at[0]))
        )
    ]
    for load in loads:
        load.start()

    fast_peers = [a * fast + lax.rem(b + j, fast) for j in range(1, fast)]
    slow_peers = [lax.rem(a + i, slow) * fast + b for i in range(1, slow)]

    def fast_peer(j):
        return fast_peers[j - 1]

    def slow_peer(i):
        return slow_peers[i - 1]

    def at_dom(member):
        return (member, gx, gy)

    at_prev, at_next = (me, gx_prev, gy), (me, gx_next, gy)
    at_left, at_right = (me, gx, gy - 1), (me, gx, gy + 1)

    barrier = pltpu.get_barrier_semaphore()
    for j in range(1, fast):
        pl.semaphore_signal(barrier, inc=1, device_id=at_dom(fast_peer(j)), device_id_type=MESH)
    for i in range(1, slow):
        pl.semaphore_signal(barrier, inc=1, device_id=at_dom(slow_peer(i)), device_id_type=MESH)
    for there in (at_next, at_prev):
        pl.semaphore_signal(barrier, inc=1, device_id=there, device_id_type=MESH)

    @pl.when(has_left)
    def _():
        pl.semaphore_signal(barrier, inc=1, device_id=at_left, device_id_type=MESH)

    @pl.when(has_right)
    def _():
        pl.semaphore_signal(barrier, inc=1, device_id=at_right, device_id_type=MESH)

    around = has_left.astype(jnp.int32) + has_right.astype(jnp.int32)
    pl.semaphore_wait(barrier, fast - 1 + slow - 1 + 2 + around)

    def part(c):
        return pl.ds(c * CHUNK, CHUNK)

    def gather_f(j, c):
        return remote(ens_hbm.at[0, 0:PAIR, part(c)], ag_f.at[j - 1, :, part(c)],
                      agf_send.at[j - 1, c], agf_recv.at[j - 1, c], at_dom(fast_peer(j)))

    def gather_s(i, c):
        return remote(ens_hbm.at[0, PAIR:FIELDS, part(c)], ag_s.at[i - 1, :, part(c)],
                      ags_send.at[i - 1, c], ags_recv.at[i - 1, c], at_dom(slow_peer(i)))

    def onward_f(i, c):
        return remote(tx_f.at[i - 1, :, part(c)], rx_f.at[i - 1, :, part(c)],
                      txf_send.at[i - 1, c], txf_recv.at[i - 1, c], at_dom(slow_peer(i)))

    def onward_s(j, c):
        return remote(tx_s.at[j - 1, :, part(c)], rx_s.at[j - 1, :, part(c)],
                      txs_send.at[j - 1, c], txs_recv.at[j - 1, c], at_dom(fast_peer(j)))

    def row_halo(side, c):
        there = at_prev if side == 0 else at_next
        edge = slice(0, STEPS) if side == 0 else slice(rows - STEPS, rows)
        return remote(state.at[0, 0, :, part(c), edge], state.at[0, 1, :, part(c), edge],
                      hx_send.at[side, c], hx_recv.at[side, c], there)

    def drag_halo(side):
        there = at_prev if side == 0 else at_next
        edge = slice(0, STEPS) if side == 0 else slice(rows - STEPS, rows)
        return remote(drag.at[0, :, edge], drag.at[1, :, edge],
                      drag_send.at[side], drag_recv.at[side], there)

    def col_halo(step, side, c):
        there = at_right if side == 0 else at_left
        return remote(hy_out.at[step, c], hy_in.at[step, side, c],
                      hy_send.at[step, side, c], hy_recv.at[step, side, c], there)

    def write_out(c):
        return pltpu.make_async_copy(out.at[:, :, part(c)], out_hbm.at[:, :, part(c)], out_sem.at[c])

    def start_columns(step, c):
        @pl.when(has_right)
        def _():
            col_halo(step, 0, c).start()

        @pl.when(has_left)
        def _():
            col_halo(step, 1, c).start()

    def wait_columns(step, c):
        @pl.when(has_left)
        def _():
            col_halo(step, 0, c).wait_recv()

        @pl.when(has_right)
        def _():
            col_halo(step, 1, c).wait_recv()

    def start_gather(c):
        for j in range(1, fast):
            gather_f(j, c).start()
        for i in range(1, slow):
            gather_s(i, c).start()

    for c in range(chunks):
        start_gather(c)

    @pl.when(jnp.logical_not(has_left))
    def _():
        hy_in[:, 0] = jnp.zeros((STEPS, chunks, rows, cols), jnp.float32)

    @pl.when(jnp.logical_not(has_right))
    def _():
        hy_in[:, 1] = jnp.zeros((STEPS, chunks, rows, cols), jnp.float32)

    sums[...] = jnp.zeros(sums.shape, jnp.float32)
    row = lax.broadcasted_iota(jnp.int32, (rows, cols), 0)
    lane = lax.broadcasted_iota(jnp.int32, (rows, cols), 1)
    loads[0].wait()

    def sources_of(member):
        total = jnp.zeros((rows, cols), jnp.int32)
        for tx in range(rows // TILE):
            for ty in range(cols // TILE):
                here = (lane >= ty * TILE) & (lane < (ty + 1) * TILE)
                if rows > TILE:
                    here = here & (row >= tx * TILE) & (row < (tx + 1) * TILE)
                total = jnp.where(here, anc[member, tx, ty], total)
        return total

    wanted_f = [sources_of(slow_peer(i)) for i in range(1, slow)]
    wanted_s = [sources_of(fast_peer(j)) for j in range(1, fast)]
    mine = sources_of(me)
    held_f = [a * fast + lax.rem(b + fast - j, fast) for j in range(1, fast)]
    held_s = [lax.rem(a + slow - i, slow) * fast + b for i in range(1, slow)]
    from_f = []
    for i in range(1, slow):
        base = lax.rem(a + slow - i, slow) * fast
        from_f.append((mine >= base) & (mine < base + fast))
    from_s = []
    for j in range(1, fast):
        base = lax.rem(b + fast - j, fast)
        hit = mine == base
        for i in range(1, slow):
            hit = hit | (mine == base + i * fast)
        from_s.append(hit)
    for load in loads[1:]:
        load.wait()
    drag_halo(0).start()
    drag_halo(1).start()

    def pass_on(c):
        for j in range(1, fast):
            gather_f(j, c).wait_recv()
        for i in range(1, slow):
            for f in range(PAIR):
                for kk in range(CHUNK):
                    k = c * CHUNK + kk
                    value = ens[0, f, k]
                    for j in range(1, fast):
                        value = jnp.where(wanted_f[i - 1] == held_f[j - 1], ag_f[j - 1, f, k], value)
                    tx_f[i - 1, f, k] = value
            onward_f(i, c).start()
        for i in range(1, slow):
            gather_s(i, c).wait_recv()
        for j in range(1, fast):
            for f in range(PAIR):
                for kk in range(CHUNK):
                    k = c * CHUNK + kk
                    value = ens[0, PAIR + f, k]
                    for i in range(1, slow):
                        value = jnp.where(wanted_s[j - 1] == held_s[i - 1], ag_s[i - 1, f, k], value)
                    tx_s[j - 1, f, k] = value
            onward_s(j, c).start()

    blank = jnp.zeros((rows, cols), jnp.float32)

    def place_of(tile, f, kk):
        return 2 * ((tile * FIELDS + f) * CHUNK + kk)

    couple = lane >> 1

    def pack(q, place, packed):
        turned = pltpu.roll(q, (place + 1) % cols, 1)
        return jnp.where(couple == place // 2, turned, packed)

    def resample(c):
        for i in range(1, slow):
            onward_f(i, c).wait_recv()
        for j in range(1, fast):
            onward_s(j, c).wait_recv()
        for kk in range(CHUNK):
            k = c * CHUNK + kk
            for f in range(FIELDS):
                q = ens[0, f, k]
                if f < PAIR:
                    for j in range(1, fast):
                        q = jnp.where(mine == held_f[j - 1], ag_f[j - 1, f, k], q)
                    for i in range(1, slow):
                        q = jnp.where(from_f[i - 1], rx_f[i - 1, f, k], q)
                else:
                    for i in range(1, slow):
                        q = jnp.where(mine == held_s[i - 1], ag_s[i - 1, f - PAIR, k], q)
                    for j in range(1, fast):
                        q = jnp.where(from_s[j - 1], rx_s[j - 1, f - PAIR, k], q)
                state[0, 0, f, k] = q
        row_halo(0, c).start()
        row_halo(1, c).start()

    def first_columns(c):
        row_halo(0, c).wait_recv()
        row_halo(1, c).wait_recv()
        packed = blank
        for tile in range(2):
            for f in range(FIELDS):
                for kk in range(CHUNK):
                    packed = pack(state[0, tile, f, c * CHUNK + kk], place_of(tile, f, kk), packed)
        hy_out[0, c] = packed
        start_columns(0, c)

    positions = (gy * cols + lane).astype(jnp.float32)
    coriolis = CORIO_BASE + CORIO_SLOPE * (positions + 0.5) / (n_gy * cols)
    half = 0.5 * ADVECT
    temp, salt = 0.5 * PRESS_SCALE * BUOY_TEMP, 0.5 * PRESS_SCALE * BUOY_SALT

    def advance(step, c, final):
        tiles = (0,) if final else (0, 1)
        wait_columns(step, c)
        columns = jnp.where(lane % 2 == 0, hy_in[step, 0, c], hy_in[step, 1, c])
        packed = blank
        press_x = [sums[step, t, 0] for t in tiles]
        press_y = [sums[step, t, 1] for t in tiles]
        flux = [[sums[step, t, 2 + f] for f in range(FIELDS)] for t in tiles]
        for kk in range(CHUNK):
            k = c * CHUNK + kk
            below = jnp.minimum(k + 1, levels - 1)
            mixing = eddy[jnp.minimum(k, levels - 2)]
            now = [[state[step, t, f, k] for f in range(FIELDS)] for t in (0, 1)]
            result = [[None] * FIELDS for t in tiles]
            coef = []
            for t in tiles:
                u, v = now[t][0], now[t][1]
                coef.append((DIFFUSE + half * u, DIFFUSE - half * u, DIFFUSE + half * v, DIFFUSE - half * v))
            diff_x, diff_y = [[] for t in tiles], [[] for t in tiles]
            for f in range(FIELDS):
                up = [pltpu.roll(now[t][f], 1, 0) for t in (0, 1)]
                down = [pltpu.roll(now[t][f], rows - 1, 0) for t in (0, 1)]
                for t in tiles:
                    q = now[t][f]
                    x_m = jnp.where(row == 0, up[1 - t], up[t])
                    x_p = jnp.where(row == rows - 1, down[1 - t], down[t])
                    edge = pltpu.roll(columns, cols - 1 - place_of(t, f, kk), 1)
                    y_m = pltpu.roll(jnp.where(lane == cols - 1, edge, q), 1, 1)
                    y_p = pltpu.roll(jnp.where(lane == 0, edge, q), cols - 1, 1)
                    flow = mixing * (state[step, t, f, below] - q)
                    total = (1.0 - 4.0 * DIFFUSE) * q + (flow - flux[t][f])
                    c_xm, c_xp, c_ym, c_yp = coef[t]
                    total = total + (c_xp * x_p + c_xm * x_m) + (c_yp * y_p + c_ym * y_m)
                    result[t][f] = total
                    flux[t][f] = flow
                    if f >= PAIR:
                        diff_x[t].append(x_p - x_m)
                        diff_y[t].append(y_p - y_m)
            for t in tiles:
                press_x[t] = press_x[t] + (temp * diff_x[t][0] - salt * diff_x[t][1])
                press_y[t] = press_y[t] + (temp * diff_y[t][0] - salt * diff_y[t][1])
                result[t][0] = result[t][0] + (coriolis * now[t][1] - press_x[t])
                result[t][1] = result[t][1] - (coriolis * now[t][0] + press_y[t])
                if kk == 0:
                    top = jnp.where(c == 0, WIND_SCALE, 0.0)
                    result[t][0] = result[t][0] + top * drag[t, 0]
                    result[t][1] = result[t][1] + top * drag[t, 1]
                for f in range(FIELDS):
                    if final:
                        out[0, f, k] = result[t][f]
                    else:
                        state[step + 1, t, f, k] = result[t][f]
                        packed = pack(result[t][f], place_of(t, f, kk), packed)
        for t in tiles:
            sums[step, t, 0] = press_x[t]
            sums[step, t, 1] = press_y[t]
            for f in range(FIELDS):
                sums[step, t, 2 + f] = flux[t][f]
        if final:
            write_out(c).start()
        else:
            hy_out[step + 1, c] = packed
            start_columns(step + 1, c)

    drag_halo(0).wait_recv()
    drag_halo(1).wait_recv()

    def every(body):
        def one(c, _):
            body(c)
            return 0

        lax.fori_loop(0, chunks, one, 0)

    every(pass_on)
    every(resample)

    def tick(t, _):
        def at(c, body):
            @pl.when((c >= 0) & (c < chunks))
            def _():
                body(c)

        at(t, first_columns)

        def one(step, _):
            at(t - 1 - step, lambda c: advance(step, c, False))
            return 0

        lax.fori_loop(0, STEPS - 1, one, 0)
        at(t - STEPS, lambda c: advance(STEPS - 1, c, True))
        return 0

    lax.fori_loop(0, chunks + STEPS, tick, 0)

    def drain(c, _):
        for j in range(1, fast):
            gather_f(j, c).wait_send()
            onward_s(j, c).wait_send()
        for i in range(1, slow):
            gather_s(i, c).wait_send()
            onward_f(i, c).wait_send()
        row_halo(0, c).wait_send()
        row_halo(1, c).wait_send()
        write_out(c).wait()
        for step in range(STEPS):
            @pl.when(has_right)
            def _():
                col_halo(step, 0, c).wait_send()

            @pl.when(has_left)
            def _():
                col_halo(step, 1, c).wait_send()

        return 0

    lax.fori_loop(0, chunks, drain, 0)
    drag_halo(0).wait_send()
    drag_halo(1).wait_send()


def per_device(slow, fast, n_gx, n_gy, ensemble, ancestors, particle_air_drag, eddy_diffusivity):
    levels, rows, cols = ensemble.shape[2:]
    chunks = levels // CHUNK
    block = (PAIR, levels, rows, cols)
    hbm = pl.BlockSpec(memory_space=pltpu.HBM)
    dma = pltpu.SemaphoreType.DMA
    f32 = jnp.float32
    return pl.pallas_call(
        functools.partial(kernel, slow, fast, n_gx, n_gy),
        out_shape=jax.ShapeDtypeStruct(ensemble.shape, f32),
        in_specs=[hbm] * 4,
        out_specs=hbm,
        scratch_shapes=[
            pltpu.VMEM(ensemble.shape, f32),
            pltpu.SMEM(ancestors.shape, jnp.int32),
            pltpu.VMEM((2,) + particle_air_drag.shape[1:], f32),
            pltpu.SMEM(eddy_diffusivity.shape, f32),
            pltpu.VMEM(ensemble.shape, f32),
            pltpu.VMEM((STEPS, 2, FIELDS, levels, rows, cols), f32),
            pltpu.VMEM((STEPS, 2, 2 + FIELDS, rows, cols), f32),
            pltpu.VMEM((fast - 1,) + block, f32),
            pltpu.VMEM((slow - 1,) + block, f32),
            pltpu.VMEM((slow - 1,) + block, f32),
            pltpu.VMEM((fast - 1,) + block, f32),
            pltpu.VMEM((slow - 1,) + block, f32),
            pltpu.VMEM((fast - 1,) + block, f32),
            pltpu.VMEM((STEPS, chunks, rows, cols), f32),
            pltpu.VMEM((STEPS, 2, chunks, rows, cols), f32),
            dma((4,)),
            dma((chunks,)),
            dma((fast - 1, chunks)),
            dma((fast - 1, chunks)),
            dma((slow - 1, chunks)),
            dma((slow - 1, chunks)),
            dma((slow - 1, chunks)),
            dma((slow - 1, chunks)),
            dma((fast - 1, chunks)),
            dma((fast - 1, chunks)),
            dma((2, chunks)),
            dma((2, chunks)),
            dma((STEPS, 2, chunks)),
            dma((STEPS, 2, chunks)),
            dma((2,)),
            dma((2,)),
        ],
        compiler_params=pltpu.CompilerParams(
            collective_id=0, has_side_effects=True, vmem_limit_bytes=32 * 1024 * 1024
        ),
        cost_estimate=pl.CostEstimate(
            flops=STEPS * 60 * math.prod(ensemble.shape),
            bytes_accessed=8 * math.prod(ensemble.shape),
            transcendentals=0,
        ),
    )(ensemble, ancestors, particle_air_drag, eddy_diffusivity)


def solution(mesh):
    members = mesh.shape["dom"]
    fast = max(n for n in range(1, math.isqrt(members) + 1) if members % n == 0)
    placed = (
        P("dom", None, None, "gx", "gy"),
        P(None, "gx", "gy"),
        P("dom", None, "gx", "gy"),
        P(),
    )
    return jax.shard_map(
        functools.partial(
            per_device, members // fast, fast, mesh.shape["gx"], mesh.shape["gy"]
        ),
        mesh=mesh,
        in_specs=placed,
        out_specs=P("dom", None, None, "gx", "gy"),
        check_vma=False,
    )
```

```python
import functools
import math

import jax
import jax.numpy as jnp
from jax import lax
from jax.experimental import pallas as pl
from jax.experimental.pallas import tpu as pltpu
from jax.sharding import PartitionSpec as P

STEPS = 4
TILE = 8
CHUNK = 4

ADVECT = 0.2
DIFFUSE = 0.15
BUOY_TEMP = 0.2
BUOY_SALT = 0.1
PRESS_SCALE = 0.25
WIND_SCALE = 0.2
CORIO_BASE = 0.1
CORIO_SLOPE = 0.1

MESH = pl.DeviceIdType.MESH
FIELDS = 4
PAIR = 2


def remote(src, dst, send, recv, where):
    return pltpu.make_async_remote_copy(
        src_ref=src,
        dst_ref=dst,
        send_sem=send,
        recv_sem=recv,
        device_id=where,
        device_id_type=MESH,
    )


def kernel(
    slow, fast, n_gx, n_gy, ens_hbm, anc_hbm, drag_hbm, eddy_hbm, out_hbm,
    ens, anc, drag, eddy, out, state, sums, ag_f, ag_s, tx_f, tx_s, rx_f, rx_s, hy_out, hy_in,
    local_sem, out_sem, agf_send, agf_recv, ags_send, ags_recv, txf_send, txf_recv, txs_send, txs_recv,
    hx_send, hx_recv, hy_send, hy_recv, drag_send, drag_recv,
):
    levels, rows, cols = ens.shape[2:]
    chunks = levels // CHUNK
    me = lax.axis_index("dom")
    a, b = me // fast, me % fast
    gx, gy = lax.axis_index("gx"), lax.axis_index("gy")
    gx_next, gx_prev = lax.rem(gx + 1, n_gx), lax.rem(gx + n_gx - 1, n_gx)
    has_left, has_right = gy > 0, gy < n_gy - 1

    loads = [
        pltpu.make_async_copy(there, here, local_sem.at[number])
        for number, (there, here) in enumerate(
            ((anc_hbm, anc), (ens_hbm, ens), (eddy_hbm, eddy), (drag_hbm.at[0], drag.at[0]))
        )
    ]
    for load in loads:
        load.start()

    fast_peers = [a * fast + lax.rem(b + j, fast) for j in range(1, fast)]
    slow_peers = [lax.rem(a + i, slow) * fast + b for i in range(1, slow)]

    def fast_peer(j):
        return fast_peers[j - 1]

    def slow_peer(i):
        return slow_peers[i - 1]

    def at_dom(member):
        return (member, gx, gy)

    at_prev, at_next = (me, gx_prev, gy), (me, gx_next, gy)
    at_left, at_right = (me, gx, gy - 1), (me, gx, gy + 1)

    barrier = pltpu.get_barrier_semaphore()
    for j in range(1, fast):
        pl.semaphore_signal(barrier, inc=1, device_id=at_dom(fast_peer(j)), device_id_type=MESH)
    for i in range(1, slow):
        pl.semaphore_signal(barrier, inc=1, device_id=at_dom(slow_peer(i)), device_id_type=MESH)
    for there in (at_next, at_prev):
        pl.semaphore_signal(barrier, inc=1, device_id=there, device_id_type=MESH)

    @pl.when(has_left)
    def _():
        pl.semaphore_signal(barrier, inc=1, device_id=at_left, device_id_type=MESH)

    @pl.when(has_right)
    def _():
        pl.semaphore_signal(barrier, inc=1, device_id=at_right, device_id_type=MESH)

    around = has_left.astype(jnp.int32) + has_right.astype(jnp.int32)
    pl.semaphore_wait(barrier, fast - 1 + slow - 1 + 2 + around)

    def part(c):
        return pl.ds(c * CHUNK, CHUNK)

    def gather_f(j, c):
        return remote(ens_hbm.at[0, 0:PAIR, part(c)], ag_f.at[j - 1, :, part(c)],
                      agf_send.at[j - 1, c], agf_recv.at[j - 1, c], at_dom(fast_peer(j)))

    def gather_s(i, c):
        return remote(ens_hbm.at[0, PAIR:FIELDS, part(c)], ag_s.at[i - 1, :, part(c)],
                      ags_send.at[i - 1, c], ags_recv.at[i - 1, c], at_dom(slow_peer(i)))

    def onward_f(i, c):
        return remote(tx_f.at[i - 1, :, part(c)], rx_f.at[i - 1, :, part(c)],
                      txf_send.at[i - 1, c], txf_recv.at[i - 1, c], at_dom(slow_peer(i)))

    def onward_s(j, c):
        return remote(tx_s.at[j - 1, :, part(c)], rx_s.at[j - 1, :, part(c)],
                      txs_send.at[j - 1, c], txs_recv.at[j - 1, c], at_dom(fast_peer(j)))

    def row_halo(side, c):
        there = at_prev if side == 0 else at_next
        edge = slice(0, STEPS) if side == 0 else slice(rows - STEPS, rows)
        return remote(state.at[0, 0, :, part(c), edge], state.at[0, 1, :, part(c), edge],
                      hx_send.at[side, c], hx_recv.at[side, c], there)

    def drag_halo(side):
        there = at_prev if side == 0 else at_next
        edge = slice(0, STEPS) if side == 0 else slice(rows - STEPS, rows)
        return remote(drag.at[0, :, edge], drag.at[1, :, edge],
                      drag_send.at[side], drag_recv.at[side], there)

    def col_halo(step, side, c):
        there = at_right if side == 0 else at_left
        return remote(hy_out.at[step, c], hy_in.at[step, side, c],
                      hy_send.at[step, side, c], hy_recv.at[step, side, c], there)

    def write_out(c):
        return pltpu.make_async_copy(out.at[:, :, part(c)], out_hbm.at[:, :, part(c)], out_sem.at[c])

    def start_columns(step, c):
        @pl.when(has_right)
        def _():
            col_halo(step, 0, c).start()

        @pl.when(has_left)
        def _():
            col_halo(step, 1, c).start()

    def wait_columns(step, c):
        @pl.when(has_left)
        def _():
            col_halo(step, 0, c).wait_recv()

        @pl.when(has_right)
        def _():
            col_halo(step, 1, c).wait_recv()

    def start_gather(c):
        for j in range(1, fast):
            gather_f(j, c).start()
        for i in range(1, slow):
            gather_s(i, c).start()

    for c in range(chunks):
        start_gather(c)

    @pl.when(jnp.logical_not(has_left))
    def _():
        hy_in[:, 0] = jnp.zeros((STEPS, chunks, rows, cols), jnp.float32)

    @pl.when(jnp.logical_not(has_right))
    def _():
        hy_in[:, 1] = jnp.zeros((STEPS, chunks, rows, cols), jnp.float32)

    sums[...] = jnp.zeros(sums.shape, jnp.float32)
    row = lax.broadcasted_iota(jnp.int32, (rows, cols), 0)
    lane = lax.broadcasted_iota(jnp.int32, (rows, cols), 1)
    loads[0].wait()

    def sources_of(member):
        total = jnp.zeros((rows, cols), jnp.int32)
        for tx in range(rows // TILE):
            for ty in range(cols // TILE):
                here = (lane >= ty * TILE) & (lane < (ty + 1) * TILE)
                if rows > TILE:
                    here = here & (row >= tx * TILE) & (row < (tx + 1) * TILE)
                total = jnp.where(here, anc[member, tx, ty], total)
        return total

    wanted_f = [sources_of(slow_peer(i)) for i in range(1, slow)]
    wanted_s = [sources_of(fast_peer(j)) for j in range(1, fast)]
    mine = sources_of(me)
    held_f = [a * fast + lax.rem(b + fast - j, fast) for j in range(1, fast)]
    held_s = [lax.rem(a + slow - i, slow) * fast + b for i in range(1, slow)]
    from_f = []
    for i in range(1, slow):
        base = lax.rem(a + slow - i, slow) * fast
        from_f.append((mine >= base) & (mine < base + fast))
    from_s = []
    for j in range(1, fast):
        base = lax.rem(b + fast - j, fast)
        hit = mine == base
        for i in range(1, slow):
            hit = hit | (mine == base + i * fast)
        from_s.append(hit)
    for load in loads[1:]:
        load.wait()
    drag_halo(0).start()
    drag_halo(1).start()

    def pass_on(c):
        for j in range(1, fast):
            gather_f(j, c).wait_recv()
        for i in range(1, slow):
            for f in range(PAIR):
                for kk in range(CHUNK):
                    k = c * CHUNK + kk
                    value = ens[0, f, k]
                    for j in range(1, fast):
                        value = jnp.where(wanted_f[i - 1] == held_f[j - 1], ag_f[j - 1, f, k], value)
                    tx_f[i - 1, f, k] = value
            onward_f(i, c).start()
        for i in range(1, slow):
            gather_s(i, c).wait_recv()
        for j in range(1, fast):
            for f in range(PAIR):
                for kk in range(CHUNK):
                    k = c * CHUNK + kk
                    value = ens[0, PAIR + f, k]
                    for i in range(1, slow):
                        value = jnp.where(wanted_s[j - 1] == held_s[i - 1], ag_s[i - 1, f, k], value)
                    tx_s[j - 1, f, k] = value
            onward_s(j, c).start()

    blank = jnp.zeros((rows, cols), jnp.float32)

    def place_of(tile, f, kk):
        return 2 * ((tile * FIELDS + f) * CHUNK + kk)

    couple = lane >> 1

    def pack(q, place, packed):
        turned = pltpu.roll(q, (place + 1) % cols, 1)
        return jnp.where(couple == place // 2, turned, packed)

    def resample(c):
        for i in range(1, slow):
            onward_f(i, c).wait_recv()
        for j in range(1, fast):
            onward_s(j, c).wait_recv()
        for kk in range(CHUNK):
            k = c * CHUNK + kk
            for f in range(FIELDS):
                q = ens[0, f, k]
                if f < PAIR:
                    for j in range(1, fast):
                        q = jnp.where(mine == held_f[j - 1], ag_f[j - 1, f, k], q)
                    for i in range(1, slow):
                        q = jnp.where(from_f[i - 1], rx_f[i - 1, f, k], q)
                else:
                    for i in range(1, slow):
                        q = jnp.where(mine == held_s[i - 1], ag_s[i - 1, f - PAIR, k], q)
                    for j in range(1, fast):
                        q = jnp.where(from_s[j - 1], rx_s[j - 1, f - PAIR, k], q)
                state[0, 0, f, k] = q
        row_halo(0, c).start()
        row_halo(1, c).start()

    def first_columns(c):
        row_halo(0, c).wait_recv()
        row_halo(1, c).wait_recv()
        packed = blank
        for tile in range(2):
            for f in range(FIELDS):
                for kk in range(CHUNK):
                    packed = pack(state[0, tile, f, c * CHUNK + kk], place_of(tile, f, kk), packed)
        hy_out[0, c] = packed
        start_columns(0, c)

    positions = (gy * cols + lane).astype(jnp.float32)
    coriolis = CORIO_BASE + CORIO_SLOPE * (positions + 0.5) / (n_gy * cols)
    half = 0.5 * ADVECT
    temp, salt = 0.5 * PRESS_SCALE * BUOY_TEMP, 0.5 * PRESS_SCALE * BUOY_SALT

    def advance(step, c, final):
        tiles = (0,) if final else (0, 1)
        wait_columns(step, c)
        columns = jnp.where(lane % 2 == 0, hy_in[step, 0, c], hy_in[step, 1, c])
        packed = blank
        press_x = [sums[step, t, 0] for t in tiles]
        press_y = [sums[step, t, 1] for t in tiles]
        flux = [[sums[step, t, 2 + f] for f in range(FIELDS)] for t in tiles]
        for kk in range(CHUNK):
            k = c * CHUNK + kk
            below = jnp.minimum(k + 1, levels - 1)
            mixing = eddy[jnp.minimum(k, levels - 2)]
            now = [[state[step, t, f, k] for f in range(FIELDS)] for t in (0, 1)]
            result = [[None] * FIELDS for t in tiles]
            coef = []
            for t in tiles:
                u, v = now[t][0], now[t][1]
                coef.append((DIFFUSE + half * u, DIFFUSE - half * u, DIFFUSE + half * v, DIFFUSE - half * v))
            diff_x, diff_y = [[] for t in tiles], [[] for t in tiles]
            for f in range(FIELDS):
                up = [pltpu.roll(now[t][f], 1, 0) for t in (0, 1)]
                down = [pltpu.roll(now[t][f], rows - 1, 0) for t in (0, 1)]
                for t in tiles:
                    q = now[t][f]
                    x_m = jnp.where(row == 0, up[1 - t], up[t])
                    x_p = jnp.where(row == rows - 1, down[1 - t], down[t])
                    edge = pltpu.roll(columns, cols - 1 - place_of(t, f, kk), 1)
                    y_m = pltpu.roll(jnp.where(lane == cols - 1, edge, q), 1, 1)
                    y_p = pltpu.roll(jnp.where(lane == 0, edge, q), cols - 1, 1)
                    flow = mixing * (state[step, t, f, below] - q)
                    total = (1.0 - 4.0 * DIFFUSE) * q + (flow - flux[t][f])
                    c_xm, c_xp, c_ym, c_yp = coef[t]
                    total = total + (c_xp * x_p + c_xm * x_m) + (c_yp * y_p + c_ym * y_m)
                    result[t][f] = total
                    flux[t][f] = flow
                    if f >= PAIR:
                        diff_x[t].append(x_p - x_m)
                        diff_y[t].append(y_p - y_m)
            for t in tiles:
                press_x[t] = press_x[t] + (temp * diff_x[t][0] - salt * diff_x[t][1])
                press_y[t] = press_y[t] + (temp * diff_y[t][0] - salt * diff_y[t][1])
                result[t][0] = result[t][0] + (coriolis * now[t][1] - press_x[t])
                result[t][1] = result[t][1] - (coriolis * now[t][0] + press_y[t])
                if kk == 0:
                    top = jnp.where(c == 0, WIND_SCALE, 0.0)
                    result[t][0] = result[t][0] + top * drag[t, 0]
                    result[t][1] = result[t][1] + top * drag[t, 1]
                for f in range(FIELDS):
                    if final:
                        out[0, f, k] = result[t][f]
                    else:
                        state[step + 1, t, f, k] = result[t][f]
                        packed = pack(result[t][f], place_of(t, f, kk), packed)
        for t in tiles:
            sums[step, t, 0] = press_x[t]
            sums[step, t, 1] = press_y[t]
            for f in range(FIELDS):
                sums[step, t, 2 + f] = flux[t][f]
        if final:
            write_out(c).start()
        else:
            hy_out[step + 1, c] = packed
            start_columns(step + 1, c)

    drag_halo(0).wait_recv()
    drag_halo(1).wait_recv()

    def every(body):
        def one(c, _):
            body(c)
            return 0

        lax.fori_loop(0, chunks, one, 0)

    every(pass_on)
    every(resample)

    def tick(t, _):
        def at(c, body):
            @pl.when((c >= 0) & (c < chunks))
            def _():
                body(c)

        at(t, first_columns)

        def one(step, _):
            at(t - 1 - step, lambda c: advance(step, c, False))
            return 0

        lax.fori_loop(0, STEPS - 1, one, 0)
        at(t - STEPS, lambda c: advance(STEPS - 1, c, True))
        return 0

    lax.fori_loop(0, chunks + STEPS, tick, 0)

    def drain(c, _):
        for j in range(1, fast):
            gather_f(j, c).wait_send()
            onward_s(j, c).wait_send()
        for i in range(1, slow):
            gather_s(i, c).wait_send()
            onward_f(i, c).wait_send()
        row_halo(0, c).wait_send()
        row_halo(1, c).wait_send()
        write_out(c).wait()
        for step in range(STEPS):
            @pl.when(has_right)
            def _():
                col_halo(step, 0, c).wait_send()

            @pl.when(has_left)
            def _():
                col_halo(step, 1, c).wait_send()

        return 0

    lax.fori_loop(0, chunks, drain, 0)
    drag_halo(0).wait_send()
    drag_halo(1).wait_send()


def per_device(slow, fast, n_gx, n_gy, ensemble, ancestors, particle_air_drag, eddy_diffusivity):
    levels, rows, cols = ensemble.shape[2:]
    chunks = levels // CHUNK
    block = (PAIR, levels, rows, cols)
    hbm = pl.BlockSpec(memory_space=pltpu.HBM)
    dma = pltpu.SemaphoreType.DMA
    f32 = jnp.float32
    return pl.pallas_call(
        functools.partial(kernel, slow, fast, n_gx, n_gy),
        out_shape=jax.ShapeDtypeStruct(ensemble.shape, f32),
        in_specs=[hbm] * 4,
        out_specs=hbm,
        scratch_shapes=[
            pltpu.VMEM(ensemble.shape, f32),
            pltpu.SMEM(ancestors.shape, jnp.int32),
            pltpu.VMEM((2,) + particle_air_drag.shape[1:], f32),
            pltpu.SMEM(eddy_diffusivity.shape, f32),
            pltpu.VMEM(ensemble.shape, f32),
            pltpu.VMEM((STEPS, 2, FIELDS, levels, rows, cols), f32),
            pltpu.VMEM((STEPS, 2, 2 + FIELDS, rows, cols), f32),
            pltpu.VMEM((fast - 1,) + block, f32),
            pltpu.VMEM((slow - 1,) + block, f32),
            pltpu.VMEM((slow - 1,) + block, f32),
            pltpu.VMEM((fast - 1,) + block, f32),
            pltpu.VMEM((slow - 1,) + block, f32),
            pltpu.VMEM((fast - 1,) + block, f32),
            pltpu.VMEM((STEPS, chunks, rows, cols), f32),
            pltpu.VMEM((STEPS, 2, chunks, rows, cols), f32),
            dma((4,)),
            dma((chunks,)),
            dma((fast - 1, chunks)),
            dma((fast - 1, chunks)),
            dma((slow - 1, chunks)),
            dma((slow - 1, chunks)),
            dma((slow - 1, chunks)),
            dma((slow - 1, chunks)),
            dma((fast - 1, chunks)),
            dma((fast - 1, chunks)),
            dma((2, chunks)),
            dma((2, chunks)),
            dma((STEPS, 2, chunks)),
            dma((STEPS, 2, chunks)),
            dma((2,)),
            dma((2,)),
        ],
        compiler_params=pltpu.CompilerParams(
            collective_id=0, has_side_effects=True, vmem_limit_bytes=32 * 1024 * 1024
        ),
        cost_estimate=pl.CostEstimate(
            flops=STEPS * 60 * math.prod(ensemble.shape),
            bytes_accessed=8 * math.prod(ensemble.shape),
            transcendentals=0,
        ),
    )(ensemble, ancestors, particle_air_drag, eddy_diffusivity)


def solution(mesh):
    members = mesh.shape["dom"]
    fast = max(n for n in range(1, math.isqrt(members) + 1) if members % n == 0)
    placed = (
        P("dom", None, None, "gx", "gy"),
        P(None, "gx", "gy"),
        P("dom", None, "gx", "gy"),
        P(),
    )
    return jax.shard_map(
        functools.partial(
            per_device, members // fast, fast, mesh.shape["gx"], mesh.shape["gy"]
        ),
        mesh=mesh,
        in_specs=placed,
        out_specs=P("dom", None, None, "gx", "gy"),
        check_vma=False,
    )
```

```python
import functools
import math

import jax
import jax.numpy as jnp
from jax import lax
from jax.experimental import pallas as pl
from jax.experimental.pallas import tpu as pltpu
from jax.sharding import PartitionSpec as P

STEPS = 4
TILE = 8
CHUNK = 8
AHEAD = 2

ADVECT = 0.2
DIFFUSE = 0.15
BUOY_TEMP = 0.2
BUOY_SALT = 0.1
PRESS_SCALE = 0.25
WIND_SCALE = 0.2
CORIO_BASE = 0.1
CORIO_SLOPE = 0.1

MESH = pl.DeviceIdType.MESH
FIELDS = 4
PAIR = 2


def remote(src, dst, send, recv, where):
    return pltpu.make_async_remote_copy(
        src_ref=src,
        dst_ref=dst,
        send_sem=send,
        recv_sem=recv,
        device_id=where,
        device_id_type=MESH,
    )


def kernel(
    slow, fast, n_gx, n_gy, ens_hbm, anc_hbm, drag_hbm, eddy_hbm, out_hbm,
    ens, anc, drag, eddy, out, state, sums, ag_f, ag_s, tx_f, tx_s, rx_f, rx_s, hy_out, hy_in,
    local_sem, out_sem, agf_send, agf_recv, ags_send, ags_recv, txf_send, txf_recv, txs_send, txs_recv,
    hx_send, hx_recv, hy_send, hy_recv, drag_send, drag_recv,
):
    levels, rows, cols = ens.shape[2:]
    chunks = levels // CHUNK
    me = lax.axis_index("dom")
    a, b = me // fast, me % fast
    gx, gy = lax.axis_index("gx"), lax.axis_index("gy")
    gx_next, gx_prev = lax.rem(gx + 1, n_gx), lax.rem(gx + n_gx - 1, n_gx)
    has_left, has_right = gy > 0, gy < n_gy - 1

    loads = [
        pltpu.make_async_copy(there, here, local_sem.at[number])
        for number, (there, here) in enumerate(
            ((anc_hbm, anc), (ens_hbm, ens), (eddy_hbm, eddy), (drag_hbm.at[0], drag.at[0]))
        )
    ]
    for load in loads:
        load.start()

    fast_peers = [a * fast + lax.rem(b + j, fast) for j in range(1, fast)]
    slow_peers = [lax.rem(a + i, slow) * fast + b for i in range(1, slow)]

    def fast_peer(j):
        return fast_peers[j - 1]

    def slow_peer(i):
        return slow_peers[i - 1]

    def at_dom(member):
        return (member, gx, gy)

    at_prev, at_next = (me, gx_prev, gy), (me, gx_next, gy)
    at_left, at_right = (me, gx, gy - 1), (me, gx, gy + 1)

    barrier = pltpu.get_barrier_semaphore()
    for j in range(1, fast):
        pl.semaphore_signal(barrier, inc=1, device_id=at_dom(fast_peer(j)), device_id_type=MESH)
    for i in range(1, slow):
        pl.semaphore_signal(barrier, inc=1, device_id=at_dom(slow_peer(i)), device_id_type=MESH)
    for there in (at_next, at_prev):
        pl.semaphore_signal(barrier, inc=1, device_id=there, device_id_type=MESH)

    @pl.when(has_left)
    def _():
        pl.semaphore_signal(barrier, inc=1, device_id=at_left, device_id_type=MESH)

    @pl.when(has_right)
    def _():
        pl.semaphore_signal(barrier, inc=1, device_id=at_right, device_id_type=MESH)

    around = has_left.astype(jnp.int32) + has_right.astype(jnp.int32)
    pl.semaphore_wait(barrier, fast - 1 + slow - 1 + 2 + around)

    def part(c):
        return pl.ds(c * CHUNK, CHUNK)

    def gather_f(j, c):
        return remote(ens_hbm.at[0, 0:PAIR, part(c)], ag_f.at[j - 1, :, part(c)],
                      agf_send.at[j - 1, c], agf_recv.at[j - 1, c], at_dom(fast_peer(j)))

    def gather_s(i, c):
        return remote(ens_hbm.at[0, PAIR:FIELDS, part(c)], ag_s.at[i - 1, :, part(c)],
                      ags_send.at[i - 1, c], ags_recv.at[i - 1, c], at_dom(slow_peer(i)))

    def onward_f(i, c):
        return remote(tx_f.at[i - 1, :, part(c)], rx_f.at[i - 1, :, part(c)],
                      txf_send.at[i - 1, c], txf_recv.at[i - 1, c], at_dom(slow_peer(i)))

    def onward_s(j, c):
        return remote(tx_s.at[j - 1, :, part(c)], rx_s.at[j - 1, :, part(c)],
                      txs_send.at[j - 1, c], txs_recv.at[j - 1, c], at_dom(fast_peer(j)))

    def row_halo(side, c):
        there = at_prev if side == 0 else at_next
        edge = slice(0, STEPS) if side == 0 else slice(rows - STEPS, rows)
        return remote(state.at[0, 0, :, part(c), edge], state.at[0, 1, :, part(c), edge],
                      hx_send.at[side, c], hx_recv.at[side, c], there)

    def drag_halo(side):
        there = at_prev if side == 0 else at_next
        edge = slice(0, STEPS) if side == 0 else slice(rows - STEPS, rows)
        return remote(drag.at[0, :, edge], drag.at[1, :, edge],
                      drag_send.at[side], drag_recv.at[side], there)

    def col_halo(step, side, c):
        there = at_right if side == 0 else at_left
        return remote(hy_out.at[step, c], hy_in.at[step, side, c],
                      hy_send.at[step, side, c], hy_recv.at[step, side, c], there)

    def write_out(c):
        return pltpu.make_async_copy(out.at[:, :, part(c)], out_hbm.at[:, :, part(c)], out_sem.at[c])

    def start_columns(step, c):
        @pl.when(has_right)
        def _():
            col_halo(step, 0, c).start()

        @pl.when(has_left)
        def _():
            col_halo(step, 1, c).start()

    def wait_columns(step, c):
        @pl.when(has_left)
        def _():
            col_halo(step, 0, c).wait_recv()

        @pl.when(has_right)
        def _():
            col_halo(step, 1, c).wait_recv()

    def start_gather(c):
        for j in range(1, fast):
            gather_f(j, c).start()
        for i in range(1, slow):
            gather_s(i, c).start()

    for c in range(min(AHEAD, chunks)):
        start_gather(c)

    @pl.when(jnp.logical_not(has_left))
    def _():
        hy_in[:, 0] = jnp.zeros((STEPS, chunks, rows, cols), jnp.float32)

    @pl.when(jnp.logical_not(has_right))
    def _():
        hy_in[:, 1] = jnp.zeros((STEPS, chunks, rows, cols), jnp.float32)

    sums[...] = jnp.zeros(sums.shape, jnp.float32)
    row = lax.broadcasted_iota(jnp.int32, (rows, cols), 0)
    lane = lax.broadcasted_iota(jnp.int32, (rows, cols), 1)
    loads[0].wait()

    def sources_of(member):
        total = jnp.zeros((rows, cols), jnp.int32)
        for tx in range(rows // TILE):
            for ty in range(cols // TILE):
                here = (lane >= ty * TILE) & (lane < (ty + 1) * TILE)
                if rows > TILE:
                    here = here & (row >= tx * TILE) & (row < (tx + 1) * TILE)
                total = jnp.where(here, anc[member, tx, ty], total)
        return total

    wanted_f = [sources_of(slow_peer(i)) for i in range(1, slow)]
    wanted_s = [sources_of(fast_peer(j)) for j in range(1, fast)]
    mine = sources_of(me)
    held_f = [a * fast + lax.rem(b + fast - j, fast) for j in range(1, fast)]
    held_s = [lax.rem(a + slow - i, slow) * fast + b for i in range(1, slow)]
    from_f = []
    for i in range(1, slow):
        base = lax.rem(a + slow - i, slow) * fast
        from_f.append((mine >= base) & (mine < base + fast))
    from_s = []
    for j in range(1, fast):
        base = lax.rem(b + fast - j, fast)
        hit = mine == base
        for i in range(1, slow):
            hit = hit | (mine == base + i * fast)
        from_s.append(hit)
    for load in loads[1:]:
        load.wait()
    drag_halo(0).start()
    drag_halo(1).start()

    def pass_on(c):
        for j in range(1, fast):
            gather_f(j, c).wait_recv()
        for i in range(1, slow):
            for f in range(PAIR):
                for kk in range(CHUNK):
                    k = c * CHUNK + kk
                    value = ens[0, f, k]
                    for j in range(1, fast):
                        value = jnp.where(wanted_f[i - 1] == held_f[j - 1], ag_f[j - 1, f, k], value)
                    tx_f[i - 1, f, k] = value
            onward_f(i, c).start()
        for i in range(1, slow):
            gather_s(i, c).wait_recv()
        for j in range(1, fast):
            for f in range(PAIR):
                for kk in range(CHUNK):
                    k = c * CHUNK + kk
                    value = ens[0, PAIR + f, k]
                    for i in range(1, slow):
                        value = jnp.where(wanted_s[j - 1] == held_s[i - 1], ag_s[i - 1, f, k], value)
                    tx_s[j - 1, f, k] = value
            onward_s(j, c).start()

        @pl.when(c + AHEAD < chunks)
        def _():
            start_gather(c + AHEAD)

    blank = jnp.zeros((rows, cols), jnp.float32)

    def place_of(tile, f, kk):
        return 2 * ((tile * FIELDS + f) * CHUNK + kk)

    couple = lane >> 1

    def pack(q, place, packed):
        turned = pltpu.roll(q, (place + 1) % cols, 1)
        return jnp.where(couple == place // 2, turned, packed)

    def resample(c):
        for i in range(1, slow):
            onward_f(i, c).wait_recv()
        for j in range(1, fast):
            onward_s(j, c).wait_recv()
        for kk in range(CHUNK):
            k = c * CHUNK + kk
            for f in range(FIELDS):
                q = ens[0, f, k]
                if f < PAIR:
                    for j in range(1, fast):
                        q = jnp.where(mine == held_f[j - 1], ag_f[j - 1, f, k], q)
                    for i in range(1, slow):
                        q = jnp.where(from_f[i - 1], rx_f[i - 1, f, k], q)
                else:
                    for i in range(1, slow):
                        q = jnp.where(mine == held_s[i - 1], ag_s[i - 1, f - PAIR, k], q)
                    for j in range(1, fast):
                        q = jnp.where(from_s[j - 1], rx_s[j - 1, f - PAIR, k], q)
                state[0, 0, f, k] = q
        row_halo(0, c).start()
        row_halo(1, c).start()

    def first_columns(c):
        row_halo(0, c).wait_recv()
        row_halo(1, c).wait_recv()
        packed = blank
        for tile in range(2):
            for f in range(FIELDS):
                for kk in range(CHUNK):
                    packed = pack(state[0, tile, f, c * CHUNK + kk], place_of(tile, f, kk), packed)
        hy_out[0, c] = packed
        start_columns(0, c)

    positions = (gy * cols + lane).astype(jnp.float32)
    coriolis = CORIO_BASE + CORIO_SLOPE * (positions + 0.5) / (n_gy * cols)
    half = 0.5 * ADVECT
    temp, salt = 0.5 * PRESS_SCALE * BUOY_TEMP, 0.5 * PRESS_SCALE * BUOY_SALT

    def advance(step, c, final):
        tiles = (0,) if final else (0, 1)
        wait_columns(step, c)
        columns = jnp.where(lane % 2 == 0, hy_in[step, 0, c], hy_in[step, 1, c])
        packed = blank
        press_x = [sums[step, t, 0] for t in tiles]
        press_y = [sums[step, t, 1] for t in tiles]
        flux = [[sums[step, t, 2 + f] for f in range(FIELDS)] for t in tiles]
        for kk in range(CHUNK):
            k = c * CHUNK + kk
            below = jnp.minimum(k + 1, levels - 1)
            mixing = eddy[jnp.minimum(k, levels - 2)]
            now = [[state[step, t, f, k] for f in range(FIELDS)] for t in (0, 1)]
            result = [[None] * FIELDS for t in tiles]
            coef = []
            for t in tiles:
                u, v = now[t][0], now[t][1]
                coef.append((DIFFUSE + half * u, DIFFUSE - half * u, DIFFUSE + half * v, DIFFUSE - half * v))
            diff_x, diff_y = [[] for t in tiles], [[] for t in tiles]
            for f in range(FIELDS):
                up = [pltpu.roll(now[t][f], 1, 0) for t in (0, 1)]
                down = [pltpu.roll(now[t][f], rows - 1, 0) for t in (0, 1)]
                for t in tiles:
                    q = now[t][f]
                    x_m = jnp.where(row == 0, up[1 - t], up[t])
                    x_p = jnp.where(row == rows - 1, down[1 - t], down[t])
                    edge = pltpu.roll(columns, cols - 1 - place_of(t, f, kk), 1)
                    y_m = pltpu.roll(jnp.where(lane == cols - 1, edge, q), 1, 1)
                    y_p = pltpu.roll(jnp.where(lane == 0, edge, q), cols - 1, 1)
                    flow = mixing * (state[step, t, f, below] - q)
                    total = (1.0 - 4.0 * DIFFUSE) * q + (flow - flux[t][f])
                    c_xm, c_xp, c_ym, c_yp = coef[t]
                    total = total + (c_xp * x_p + c_xm * x_m) + (c_yp * y_p + c_ym * y_m)
                    result[t][f] = total
                    flux[t][f] = flow
                    if f >= PAIR:
                        diff_x[t].append(x_p - x_m)
                        diff_y[t].append(y_p - y_m)
            for t in tiles:
                press_x[t] = press_x[t] + (temp * diff_x[t][0] - salt * diff_x[t][1])
                press_y[t] = press_y[t] + (temp * diff_y[t][0] - salt * diff_y[t][1])
                result[t][0] = result[t][0] + (coriolis * now[t][1] - press_x[t])
                result[t][1] = result[t][1] - (coriolis * now[t][0] + press_y[t])
                if kk == 0:
                    top = jnp.where(c == 0, WIND_SCALE, 0.0)
                    result[t][0] = result[t][0] + top * drag[t, 0]
                    result[t][1] = result[t][1] + top * drag[t, 1]
                for f in range(FIELDS):
                    if final:
                        out[0, f, k] = result[t][f]
                    else:
                        state[step + 1, t, f, k] = result[t][f]
                        packed = pack(result[t][f], place_of(t, f, kk), packed)
        for t in tiles:
            sums[step, t, 0] = press_x[t]
            sums[step, t, 1] = press_y[t]
            for f in range(FIELDS):
                sums[step, t, 2 + f] = flux[t][f]
        if final:
            write_out(c).start()
        else:
            hy_out[step + 1, c] = packed
            start_columns(step + 1, c)

    drag_halo(0).wait_recv()
    drag_halo(1).wait_recv()

    def at(c, body):
        @pl.when((c >= 0) & (c < chunks))
        def _():
            body(c)

    def exchange(t, _):
        at(t, pass_on)
        at(t - 2, resample)
        return 0

    lax.fori_loop(0, chunks + 2, exchange, 0)

    def tick(t, _):
        at(t, first_columns)

        def one(step, _):
            at(t - 1 - step, lambda c: advance(step, c, False))
            return 0

        lax.fori_loop(0, STEPS - 1, one, 0)
        at(t - STEPS, lambda c: advance(STEPS - 1, c, True))
        return 0

    lax.fori_loop(0, chunks + STEPS, tick, 0)

    def drain(c, _):
        for j in range(1, fast):
            gather_f(j, c).wait_send()
            onward_s(j, c).wait_send()
        for i in range(1, slow):
            gather_s(i, c).wait_send()
            onward_f(i, c).wait_send()
        row_halo(0, c).wait_send()
        row_halo(1, c).wait_send()
        write_out(c).wait()
        for step in range(STEPS):
            @pl.when(has_right)
            def _():
                col_halo(step, 0, c).wait_send()

            @pl.when(has_left)
            def _():
                col_halo(step, 1, c).wait_send()

        return 0

    lax.fori_loop(0, chunks, drain, 0)
    drag_halo(0).wait_send()
    drag_halo(1).wait_send()


def per_device(slow, fast, n_gx, n_gy, ensemble, ancestors, particle_air_drag, eddy_diffusivity):
    levels, rows, cols = ensemble.shape[2:]
    chunks = levels // CHUNK
    block = (PAIR, levels, rows, cols)
    hbm = pl.BlockSpec(memory_space=pltpu.HBM)
    dma = pltpu.SemaphoreType.DMA
    f32 = jnp.float32
    return pl.pallas_call(
        functools.partial(kernel, slow, fast, n_gx, n_gy),
        out_shape=jax.ShapeDtypeStruct(ensemble.shape, f32),
        in_specs=[hbm] * 4,
        out_specs=hbm,
        scratch_shapes=[
            pltpu.VMEM(ensemble.shape, f32),
            pltpu.SMEM(ancestors.shape, jnp.int32),
            pltpu.VMEM((2,) + particle_air_drag.shape[1:], f32),
            pltpu.SMEM(eddy_diffusivity.shape, f32),
            pltpu.VMEM(ensemble.shape, f32),
            pltpu.VMEM((STEPS, 2, FIELDS, levels, rows, cols), f32),
            pltpu.VMEM((STEPS, 2, 2 + FIELDS, rows, cols), f32),
            pltpu.VMEM((fast - 1,) + block, f32),
            pltpu.VMEM((slow - 1,) + block, f32),
            pltpu.VMEM((slow - 1,) + block, f32),
            pltpu.VMEM((fast - 1,) + block, f32),
            pltpu.VMEM((slow - 1,) + block, f32),
            pltpu.VMEM((fast - 1,) + block, f32),
            pltpu.VMEM((STEPS, chunks, rows, cols), f32),
            pltpu.VMEM((STEPS, 2, chunks, rows, cols), f32),
            dma((4,)),
            dma((chunks,)),
            dma((fast - 1, chunks)),
            dma((fast - 1, chunks)),
            dma((slow - 1, chunks)),
            dma((slow - 1, chunks)),
            dma((slow - 1, chunks)),
            dma((slow - 1, chunks)),
            dma((fast - 1, chunks)),
            dma((fast - 1, chunks)),
            dma((2, chunks)),
            dma((2, chunks)),
            dma((STEPS, 2, chunks)),
            dma((STEPS, 2, chunks)),
            dma((2,)),
            dma((2,)),
        ],
        compiler_params=pltpu.CompilerParams(
            collective_id=0, has_side_effects=True, vmem_limit_bytes=32 * 1024 * 1024
        ),
        cost_estimate=pl.CostEstimate(
            flops=STEPS * 60 * math.prod(ensemble.shape),
            bytes_accessed=8 * math.prod(ensemble.shape),
            transcendentals=0,
        ),
    )(ensemble, ancestors, particle_air_drag, eddy_diffusivity)


def solution(mesh):
    members = mesh.shape["dom"]
    fast = max(n for n in range(1, math.isqrt(members) + 1) if members % n == 0)
    placed = (
        P("dom", None, None, "gx", "gy"),
        P(None, "gx", "gy"),
        P("dom", None, "gx", "gy"),
        P(),
    )
    return jax.shard_map(
        functools.partial(
            per_device, members // fast, fast, mesh.shape["gx"], mesh.shape["gy"]
        ),
        mesh=mesh,
        in_specs=placed,
        out_specs=P("dom", None, None, "gx", "gy"),
        check_vma=False,
    )
```

```python
import functools
import math

import jax
import jax.numpy as jnp
from jax import lax
from jax.experimental import pallas as pl
from jax.experimental.pallas import tpu as pltpu
from jax.sharding import PartitionSpec as P

STEPS = 4
TILE = 8
CHUNK = 8
AHEAD = 2

ADVECT = 0.2
DIFFUSE = 0.15
BUOY_TEMP = 0.2
BUOY_SALT = 0.1
PRESS_SCALE = 0.25
WIND_SCALE = 0.2
CORIO_BASE = 0.1
CORIO_SLOPE = 0.1

MESH = pl.DeviceIdType.MESH
FIELDS = 4
PAIR = 2


def remote(src, dst, send, recv, where):
    return pltpu.make_async_remote_copy(
        src_ref=src,
        dst_ref=dst,
        send_sem=send,
        recv_sem=recv,
        device_id=where,
        device_id_type=MESH,
    )


def kernel(
    slow, fast, n_gx, n_gy, ens_hbm, anc_hbm, drag_hbm, eddy_hbm, out,
    ens, anc, drag, eddy, state, sums, ag_f, ag_s, tx_f, tx_s, rx_f, rx_s, hy_out, hy_in,
    local_sem, agf_send, agf_recv, ags_send, ags_recv, txf_send, txf_recv, txs_send, txs_recv,
    hx_send, hx_recv, hy_send, hy_recv, drag_send, drag_recv,
):
    levels, rows, cols = ens.shape[2:]
    chunks = levels // CHUNK
    me = lax.axis_index("dom")
    a, b = me // fast, me % fast
    gx, gy = lax.axis_index("gx"), lax.axis_index("gy")
    gx_next, gx_prev = lax.rem(gx + 1, n_gx), lax.rem(gx + n_gx - 1, n_gx)
    has_left, has_right = gy > 0, gy < n_gy - 1

    loads = [
        pltpu.make_async_copy(there, here, local_sem.at[number])
        for number, (there, here) in enumerate(
            ((anc_hbm, anc), (ens_hbm, ens), (eddy_hbm, eddy), (drag_hbm.at[0], drag.at[0]))
        )
    ]
    for load in loads:
        load.start()

    fast_peers = [a * fast + lax.rem(b + j, fast) for j in range(1, fast)]
    slow_peers = [lax.rem(a + i, slow) * fast + b for i in range(1, slow)]

    def fast_peer(j):
        return fast_peers[j - 1]

    def slow_peer(i):
        return slow_peers[i - 1]

    def at_dom(member):
        return (member, gx, gy)

    at_prev, at_next = (me, gx_prev, gy), (me, gx_next, gy)
    at_left, at_right = (me, gx, gy - 1), (me, gx, gy + 1)

    barrier = pltpu.get_barrier_semaphore()
    for j in range(1, fast):
        pl.semaphore_signal(barrier, inc=1, device_id=at_dom(fast_peer(j)), device_id_type=MESH)
    for i in range(1, slow):
        pl.semaphore_signal(barrier, inc=1, device_id=at_dom(slow_peer(i)), device_id_type=MESH)
    for there in (at_next, at_prev):
        pl.semaphore_signal(barrier, inc=1, device_id=there, device_id_type=MESH)

    @pl.when(has_left)
    def _():
        pl.semaphore_signal(barrier, inc=1, device_id=at_left, device_id_type=MESH)

    @pl.when(has_right)
    def _():
        pl.semaphore_signal(barrier, inc=1, device_id=at_right, device_id_type=MESH)

    around = has_left.astype(jnp.int32) + has_right.astype(jnp.int32)
    pl.semaphore_wait(barrier, fast - 1 + slow - 1 + 2 + around)

    def part(c):
        return pl.ds(c * CHUNK, CHUNK)

    def gather_f(j, c):
        return remote(ens_hbm.at[0, 0:PAIR, part(c)], ag_f.at[j - 1, :, part(c)],
                      agf_send.at[j - 1, c], agf_recv.at[j - 1, c], at_dom(fast_peer(j)))

    def gather_s(i, c):
        return remote(ens_hbm.at[0, PAIR:FIELDS, part(c)], ag_s.at[i - 1, :, part(c)],
                      ags_send.at[i - 1, c], ags_recv.at[i - 1, c], at_dom(slow_peer(i)))

    def onward_f(i, c):
        return remote(tx_f.at[i - 1, :, part(c)], rx_f.at[i - 1, :, part(c)],
                      txf_send.at[i - 1, c], txf_recv.at[i - 1, c], at_dom(slow_peer(i)))

    def onward_s(j, c):
        return remote(tx_s.at[j - 1, :, part(c)], rx_s.at[j - 1, :, part(c)],
                      txs_send.at[j - 1, c], txs_recv.at[j - 1, c], at_dom(fast_peer(j)))

    def row_halo(side, c):
        there = at_prev if side == 0 else at_next
        edge = slice(0, STEPS) if side == 0 else slice(rows - STEPS, rows)
        return remote(state.at[0, 0, :, part(c), edge], state.at[0, 1, :, part(c), edge],
                      hx_send.at[side, c], hx_recv.at[side, c], there)

    def drag_halo(side):
        there = at_prev if side == 0 else at_next
        edge = slice(0, STEPS) if side == 0 else slice(rows - STEPS, rows)
        return remote(drag.at[0, :, edge], drag.at[1, :, edge],
                      drag_send.at[side], drag_recv.at[side], there)

    def col_halo(step, side, c):
        there = at_right if side == 0 else at_left
        return remote(hy_out.at[step, c], hy_in.at[step, side, c],
                      hy_send.at[step, side, c], hy_recv.at[step, side, c], there)

    def start_columns(step, c):
        @pl.when(has_right)
        def _():
            col_halo(step, 0, c).start()

        @pl.when(has_left)
        def _():
            col_halo(step, 1, c).start()

    def wait_columns(step, c):
        @pl.when(has_left)
        def _():
            col_halo(step, 0, c).wait_recv()

        @pl.when(has_right)
        def _():
            col_halo(step, 1, c).wait_recv()

    def start_gather(c):
        for j in range(1, fast):
            gather_f(j, c).start()
        for i in range(1, slow):
            gather_s(i, c).start()

    for c in range(min(AHEAD, chunks)):
        start_gather(c)

    @pl.when(jnp.logical_not(has_left))
    def _():
        hy_in[:, 0] = jnp.zeros((STEPS, chunks, rows, cols), jnp.float32)

    @pl.when(jnp.logical_not(has_right))
    def _():
        hy_in[:, 1] = jnp.zeros((STEPS, chunks, rows, cols), jnp.float32)

    sums[...] = jnp.zeros(sums.shape, jnp.float32)
    row = lax.broadcasted_iota(jnp.int32, (rows, cols), 0)
    lane = lax.broadcasted_iota(jnp.int32, (rows, cols), 1)
    loads[0].wait()

    def sources_of(member):
        total = jnp.zeros((rows, cols), jnp.int32)
        for tx in range(rows // TILE):
            for ty in range(cols // TILE):
                here = (lane >= ty * TILE) & (lane < (ty + 1) * TILE)
                if rows > TILE:
                    here = here & (row >= tx * TILE) & (row < (tx + 1) * TILE)
                total = jnp.where(here, anc[member, tx, ty], total)
        return total

    wanted_f = [sources_of(slow_peer(i)) for i in range(1, slow)]
    wanted_s = [sources_of(fast_peer(j)) for j in range(1, fast)]
    mine = sources_of(me)
    held_f = [a * fast + lax.rem(b + fast - j, fast) for j in range(1, fast)]
    held_s = [lax.rem(a + slow - i, slow) * fast + b for i in range(1, slow)]
    from_f = []
    for i in range(1, slow):
        base = lax.rem(a + slow - i, slow) * fast
        from_f.append((mine >= base) & (mine < base + fast))
    from_s = []
    for j in range(1, fast):
        base = lax.rem(b + fast - j, fast)
        hit = mine == base
        for i in range(1, slow):
            hit = hit | (mine == base + i * fast)
        from_s.append(hit)
    for load in loads[1:]:
        load.wait()
    drag_halo(0).start()
    drag_halo(1).start()

    def pass_on(c):
        for j in range(1, fast):
            gather_f(j, c).wait_recv()
        for i in range(1, slow):
            for f in range(PAIR):
                for kk in range(CHUNK):
                    k = c * CHUNK + kk
                    value = ens[0, f, k]
                    for j in range(1, fast):
                        value = jnp.where(wanted_f[i - 1] == held_f[j - 1], ag_f[j - 1, f, k], value)
                    tx_f[i - 1, f, k] = value
            onward_f(i, c).start()
        for i in range(1, slow):
            gather_s(i, c).wait_recv()
        for j in range(1, fast):
            for f in range(PAIR):
                for kk in range(CHUNK):
                    k = c * CHUNK + kk
                    value = ens[0, PAIR + f, k]
                    for i in range(1, slow):
                        value = jnp.where(wanted_s[j - 1] == held_s[i - 1], ag_s[i - 1, f, k], value)
                    tx_s[j - 1, f, k] = value
            onward_s(j, c).start()

        @pl.when(c + AHEAD < chunks)
        def _():
            start_gather(c + AHEAD)

    blank = jnp.zeros((rows, cols), jnp.float32)

    def place_of(tile, f, kk):
        return 2 * ((tile * FIELDS + f) * CHUNK + kk)

    couple = lane >> 1

    def pack(q, place, packed):
        turned = pltpu.roll(q, (place + 1) % cols, 1)
        return jnp.where(couple == place // 2, turned, packed)

    def resample(c):
        for i in range(1, slow):
            onward_f(i, c).wait_recv()
        for j in range(1, fast):
            onward_s(j, c).wait_recv()
        for kk in range(CHUNK):
            k = c * CHUNK + kk
            for f in range(FIELDS):
                q = ens[0, f, k]
                if f < PAIR:
                    for j in range(1, fast):
                        q = jnp.where(mine == held_f[j - 1], ag_f[j - 1, f, k], q)
                    for i in range(1, slow):
                        q = jnp.where(from_f[i - 1], rx_f[i - 1, f, k], q)
                else:
                    for i in range(1, slow):
                        q = jnp.where(mine == held_s[i - 1], ag_s[i - 1, f - PAIR, k], q)
                    for j in range(1, fast):
                        q = jnp.where(from_s[j - 1], rx_s[j - 1, f - PAIR, k], q)
                state[0, 0, f, k] = q
        row_halo(0, c).start()
        row_halo(1, c).start()

    def first_columns(c):
        row_halo(0, c).wait_recv()
        row_halo(1, c).wait_recv()
        packed = blank
        for tile in range(2):
            for f in range(FIELDS):
                for kk in range(CHUNK):
                    packed = pack(state[0, tile, f, c * CHUNK + kk], place_of(tile, f, kk), packed)
        hy_out[0, c] = packed
        start_columns(0, c)

    positions = (gy * cols + lane).astype(jnp.float32)
    coriolis = CORIO_BASE + CORIO_SLOPE * (positions + 0.5) / (n_gy * cols)
    half = 0.5 * ADVECT
    temp, salt = 0.5 * PRESS_SCALE * BUOY_TEMP, 0.5 * PRESS_SCALE * BUOY_SALT

    def advance(step, c, final):
        tiles = (0,) if final else (0, 1)
        wait_columns(step, c)
        columns = jnp.where(lane % 2 == 0, hy_in[step, 0, c], hy_in[step, 1, c])
        packed = blank
        press_x = [sums[step, t, 0] for t in tiles]
        press_y = [sums[step, t, 1] for t in tiles]
        flux = [[sums[step, t, 2 + f] for f in range(FIELDS)] for t in tiles]
        for kk in range(CHUNK):
            k = c * CHUNK + kk
            below = jnp.minimum(k + 1, levels - 1)
            mixing = eddy[jnp.minimum(k, levels - 2)]
            now = [[state[step, t, f, k] for f in range(FIELDS)] for t in (0, 1)]
            result = [[None] * FIELDS for t in tiles]
            coef = []
            for t in tiles:
                u, v = now[t][0], now[t][1]
                coef.append((DIFFUSE + half * u, DIFFUSE - half * u, DIFFUSE + half * v, DIFFUSE - half * v))
            diff_x, diff_y = [[] for t in tiles], [[] for t in tiles]
            for f in range(FIELDS):
                up = [pltpu.roll(now[t][f], 1, 0) for t in (0, 1)]
                down = [pltpu.roll(now[t][f], rows - 1, 0) for t in (0, 1)]
                for t in tiles:
                    q = now[t][f]
                    x_m = jnp.where(row == 0, up[1 - t], up[t])
                    x_p = jnp.where(row == rows - 1, down[1 - t], down[t])
                    edge = pltpu.roll(columns, cols - 1 - place_of(t, f, kk), 1)
                    y_m = pltpu.roll(jnp.where(lane == cols - 1, edge, q), 1, 1)
                    y_p = pltpu.roll(jnp.where(lane == 0, edge, q), cols - 1, 1)
                    flow = mixing * (state[step, t, f, below] - q)
                    total = (1.0 - 4.0 * DIFFUSE) * q + (flow - flux[t][f])
                    c_xm, c_xp, c_ym, c_yp = coef[t]
                    total = total + (c_xp * x_p + c_xm * x_m) + (c_yp * y_p + c_ym * y_m)
                    result[t][f] = total
                    flux[t][f] = flow
                    if f >= PAIR:
                        diff_x[t].append(x_p - x_m)
                        diff_y[t].append(y_p - y_m)
            for t in tiles:
                press_x[t] = press_x[t] + (temp * diff_x[t][0] - salt * diff_x[t][1])
                press_y[t] = press_y[t] + (temp * diff_y[t][0] - salt * diff_y[t][1])
                result[t][0] = result[t][0] + (coriolis * now[t][1] - press_x[t])
                result[t][1] = result[t][1] - (coriolis * now[t][0] + press_y[t])
                if kk == 0:
                    top = jnp.where(c == 0, WIND_SCALE, 0.0)
                    result[t][0] = result[t][0] + top * drag[t, 0]
                    result[t][1] = result[t][1] + top * drag[t, 1]
                for f in range(FIELDS):
                    if final:
                        out[0, f, k] = result[t][f]
                    else:
                        state[step + 1, t, f, k] = result[t][f]
                        packed = pack(result[t][f], place_of(t, f, kk), packed)
        for t in tiles:
            sums[step, t, 0] = press_x[t]
            sums[step, t, 1] = press_y[t]
            for f in range(FIELDS):
                sums[step, t, 2 + f] = flux[t][f]
        if not final:
            hy_out[step + 1, c] = packed
            start_columns(step + 1, c)

    drag_halo(0).wait_recv()
    drag_halo(1).wait_recv()

    def at(c, body):
        @pl.when((c >= 0) & (c < chunks))
        def _():
            body(c)

    def exchange(t, _):
        at(t, pass_on)
        at(t - 2, resample)
        return 0

    lax.fori_loop(0, chunks + 2, exchange, 0)

    def tick(t, _):
        at(t, first_columns)

        def one(step, _):
            at(t - 1 - step, lambda c: advance(step, c, False))
            return 0

        lax.fori_loop(0, STEPS - 1, one, 0)
        at(t - STEPS, lambda c: advance(STEPS - 1, c, True))
        return 0

    lax.fori_loop(0, chunks + STEPS, tick, 0)

    def drain(c, _):
        for j in range(1, fast):
            gather_f(j, c).wait_send()
            onward_s(j, c).wait_send()
        for i in range(1, slow):
            gather_s(i, c).wait_send()
            onward_f(i, c).wait_send()
        row_halo(0, c).wait_send()
        row_halo(1, c).wait_send()
        for step in range(STEPS):
            @pl.when(has_right)
            def _():
                col_halo(step, 0, c).wait_send()

            @pl.when(has_left)
            def _():
                col_halo(step, 1, c).wait_send()

        return 0

    lax.fori_loop(0, chunks, drain, 0)
    drag_halo(0).wait_send()
    drag_halo(1).wait_send()


def per_device(slow, fast, n_gx, n_gy, ensemble, ancestors, particle_air_drag, eddy_diffusivity):
    levels, rows, cols = ensemble.shape[2:]
    chunks = levels // CHUNK
    block = (PAIR, levels, rows, cols)
    hbm = pl.BlockSpec(memory_space=pltpu.HBM)
    dma = pltpu.SemaphoreType.DMA
    f32 = jnp.float32
    return pl.pallas_call(
        functools.partial(kernel, slow, fast, n_gx, n_gy),
        out_shape=jax.ShapeDtypeStruct(ensemble.shape, f32),
        in_specs=[hbm] * 4,
        out_specs=pl.BlockSpec(memory_space=pltpu.VMEM),
        scratch_shapes=[
            pltpu.VMEM(ensemble.shape, f32),
            pltpu.SMEM(ancestors.shape, jnp.int32),
            pltpu.VMEM((2,) + particle_air_drag.shape[1:], f32),
            pltpu.SMEM(eddy_diffusivity.shape, f32),
            pltpu.VMEM((STEPS, 2, FIELDS, levels, rows, cols), f32),
            pltpu.VMEM((STEPS, 2, 2 + FIELDS, rows, cols), f32),
            pltpu.VMEM((fast - 1,) + block, f32),
            pltpu.VMEM((slow - 1,) + block, f32),
            pltpu.VMEM((slow - 1,) + block, f32),
            pltpu.VMEM((fast - 1,) + block, f32),
            pltpu.VMEM((slow - 1,) + block, f32),
            pltpu.VMEM((fast - 1,) + block, f32),
            pltpu.VMEM((STEPS, chunks, rows, cols), f32),
            pltpu.VMEM((STEPS, 2, chunks, rows, cols), f32),
            dma((4,)),
            dma((fast - 1, chunks)),
            dma((fast - 1, chunks)),
            dma((slow - 1, chunks)),
            dma((slow - 1, chunks)),
            dma((slow - 1, chunks)),
            dma((slow - 1, chunks)),
            dma((fast - 1, chunks)),
            dma((fast - 1, chunks)),
            dma((2, chunks)),
            dma((2, chunks)),
            dma((STEPS, 2, chunks)),
            dma((STEPS, 2, chunks)),
            dma((2,)),
            dma((2,)),
        ],
        compiler_params=pltpu.CompilerParams(
            collective_id=0, has_side_effects=True, vmem_limit_bytes=32 * 1024 * 1024
        ),
        cost_estimate=pl.CostEstimate(
            flops=STEPS * 60 * math.prod(ensemble.shape),
            bytes_accessed=8 * math.prod(ensemble.shape),
            transcendentals=0,
        ),
    )(ensemble, ancestors, particle_air_drag, eddy_diffusivity)


def solution(mesh):
    members = mesh.shape["dom"]
    fast = max(n for n in range(1, math.isqrt(members) + 1) if members % n == 0)
    placed = (
        P("dom", None, None, "gx", "gy"),
        P(None, "gx", "gy"),
        P("dom", None, "gx", "gy"),
        P(),
    )
    return jax.shard_map(
        functools.partial(
            per_device, members // fast, fast, mesh.shape["gx"], mesh.shape["gy"]
        ),
        mesh=mesh,
        in_specs=placed,
        out_specs=P("dom", None, None, "gx", "gy"),
        check_vma=False,
    )
```
